512 devices in a mesh: dp: 16 (over y, x), tp: 32 (over z, core).
Axes of the slice: x: 4, y: 4, z: 16, core: 2. Of those that a mesh axis runs over, the one named last changes fastest.
Arguments:
- token_codes: bfloat16 [8192, 3584], P(('dp', 'tp')), parts along dimension 0, may hold values from -127 to 127
- token_scales: bfloat16 [8192], P(('dp', 'tp')), parts along dimension 0, may hold values from 0.0049743652 to 0.049804688
- live_counts: int32 [512], P(('dp', 'tp')), parts along dimension 0, may hold values from 0 to 16, as said below
- gate_codes: bfloat16 [3584, 9216], P(None, 'tp'), may hold values from -127 to 127
- up_codes: bfloat16 [3584, 9216], P(None, 'tp'), may hold values from -127 to 127
- gate_scales: float32 [9216], P('tp'), may hold values from 2e-05 to 0.0018
- up_scales: float32 [9216], P('tp'), may hold values from 2e-05 to 0.0018
Outputs:
- down_input: bfloat16 [8192, 9216], P('dp', 'tp'), parts along dimension 0
- row_peak: float32 [8192], P('dp'), parts along dimension 0
The draws below stay inside these ranges and needn't reach their ends.
There are 16 independent parts, one for each index of `dp`. The reference program is written for one: setup_inputs(seed, part) draws one part's arguments, and reference() takes and returns one part's arrays. A program takes and returns all parts, laid end to end along the dimension named above; an argument that names none is the same for every part. Nothing has to cross between parts.
Inputs may be any that keep to these rules, and one draw needn't show every extreme that they name: `live_counts`: the counts of one group sum to exactly 256, and some device of every group holds 16.
All inputs are finite; a program needn't handle non-finite values. Where the reference program divides by a largest or mean magnitude, that divisor is 1e-20 or more.
Results may differ from the reference program's by a relative error of at most 0.014.
Values may be sent and summed in bfloat16 or wider, within the bound.
A program may use at most 64 MiB of HBM per device.

```python
import math
import jax
import jax.numpy as jnp

D = 3584
FF = 9216
R_MAX = 16
ROWS = 512
N_TP = 32


def integer_codes(key, rows_count, cols_count):
    values = jax.random.randint(key, (rows_count, cols_count), -127, 128)
    return values.astype(jnp.float32).astype(jnp.bfloat16)


def real_codes(key, rows_count, cols_count):
    first_key = jax.random.fold_in(key, 0)
    values = jax.random.uniform(first_key, (rows_count, cols_count), jnp.float32, -127.0, 127.0)
    return values.astype(jnp.bfloat16)


def channel_scales(key):
    uniform_part = jax.random.uniform(key, (FF,), jnp.float32)
    values = 2e-05 * jnp.power(90.0, uniform_part)
    return values.astype(jnp.float32)


def draw_token_codes(key, part):
    key = jax.random.fold_in(key, 2)
    return real_codes(key, ROWS, D)


def draw_gate_codes(key, part):
    key = jax.random.fold_in(key, 3)
    return integer_codes(key, D, FF)


def draw_up_codes(key, part):
    key = jax.random.fold_in(key, 4)
    return integer_codes(key, D, FF)


def draw_gate_scales(key, part):
    key = jax.random.fold_in(key, 5)
    return channel_scales(key)


def draw_up_scales(key, part):
    key = jax.random.fold_in(key, 6)
    return channel_scales(key)


def draw_live_counts(key, part):
    key = jax.random.fold_in(key, 1)
    first_key, second_key = jax.random.split(key)
    half_count = N_TP // 2
    first_half = jax.random.randint(first_key, (half_count,), 0, R_MAX + 1)
    first_half = first_half.at[0].set(R_MAX)
    paired = jnp.concatenate([first_half, R_MAX - first_half])
    shuffle = jax.random.permutation(second_key, N_TP)
    return paired[shuffle].astype(jnp.int32)


def level_of(key, dims, pieces, least, high):
    factor_of, own = 1.0, jax.random.fold_in(key, 6)
    for position, blocks in pieces:
        draws = jnp.exp(jax.random.uniform(jax.random.fold_in(own, position), (blocks,), jnp.float32, least / len(pieces), high / len(pieces)))
        factor_of = factor_of * jnp.repeat(draws, dims[position] // blocks).reshape([-1 if axis == position else 1 for axis in range(len(dims))])
    return factor_of


def setup_inputs(seed: int = 0, part: int = 0) -> dict:
    key_list = jax.random.split(jax.random.key(seed), 8)
    part_keys = jax.random.split(jax.random.fold_in(key_list[7], part), 8)
    return {
        "token_codes": draw_token_codes(jax.random.fold_in(jax.random.fold_in(key_list[7], part), 71), part),
        "token_scales": jnp.clip(jnp.exp(math.log(0.049804688) - 2.3038113 * jax.random.uniform(part_keys[1], (ROWS,), jnp.float32) ** level_of(part_keys[1], (ROWS,), ((0, 32),), -0.2, 0.2)), 0.0049743652, 0.049804688).astype(jnp.bfloat16),
        "live_counts": draw_live_counts(jax.random.fold_in(jax.random.fold_in(key_list[7], part), 71), part),
        "gate_codes": draw_gate_codes(jax.random.fold_in(key_list[7], 71), part),
        "up_codes": draw_up_codes(jax.random.fold_in(key_list[7], 71), part),
        "gate_scales": draw_gate_scales(jax.random.fold_in(key_list[7], 71), part),
        "up_scales": draw_up_scales(jax.random.fold_in(key_list[7], 71), part),
    }


def reference(token_codes, token_scales, live_counts, gate_codes, up_codes, gate_scales, up_scales):
    row_ids = jnp.arange(ROWS).astype(jnp.int32)
    owner_ids = row_ids // R_MAX
    slot_ids = row_ids % R_MAX
    alive_rows = slot_ids < live_counts[owner_ids]
    scale_col = token_scales.astype(jnp.float32)[:, None]
    gate_acc = jnp.dot(token_codes, gate_codes, preferred_element_type=jnp.float32)
    up_acc = jnp.dot(token_codes, up_codes, preferred_element_type=jnp.float32)
    gate_value = gate_acc * scale_col * gate_scales[None, :]
    up_value = up_acc * scale_col * up_scales[None, :]
    product = jax.nn.silu(gate_value) * up_value
    hidden = jnp.where(alive_rows[:, None], product, jnp.zeros_like(product)).astype(jnp.bfloat16)
    wide = hidden.astype(jnp.float32)
    row_peak = jnp.maximum(jnp.max(jnp.abs(wide), axis=1), 1e-5)
    down_input = (wide / row_peak[:, None]).astype(jnp.bfloat16)
    return down_input, row_peak
```

```python
import functools

import jax
import jax.numpy as jnp
from jax import lax
from jax.experimental import pallas as pl
from jax.experimental.pallas import tpu as pltpu
from jax.sharding import PartitionSpec as P

MESH = pl.DeviceIdType.MESH
SLOTS = 16
PIECES = 4
LANES = 128


def kernel(
    tp, width, hidden_units,
    codes_hbm, scales_ref, counts_ref, gate_hbm, up_hbm, gate_scales_ref, up_scales_ref,
    hidden_ref, peaks_ref,
    rows_buf, gate_buf, up_buf, local_peaks, own_peaks, all_peaks,
    send_sem, recv_sem, sib_send, sib_recv, peak_send, peak_recv, load_sem,
):
    me = lax.axis_index("tp")
    chips = tp // 2
    far = chips // 2
    sibling = me + 1 - 2 * lax.rem(me, 2)
    chip = me // 2
    row_count = tp * SLOTS
    full = width + LANES

    def at(distance):
        return lax.rem(me + 2 * distance + 2 * tp, tp)

    def rows_of(device):
        return pl.ds(pl.multiple_of(device * SLOTS, SLOTS), SLOTS)

    def chip_rows(distance):
        start = lax.rem(chip + distance + chips, chips) * (2 * SLOTS)
        return pl.ds(pl.multiple_of(start, 2 * SLOTS), 2 * SLOTS)

    tiles = full // LANES
    edges = [(tiles * s) // PIECES * LANES for s in range(PIECES + 1)]
    piece = [pl.ds(a, b - a) for a, b in zip(edges[:-1], edges[1:])]
    signs = (1, -1)

    barrier = pltpu.get_barrier_semaphore()
    for device in (at(1), at(-1), sibling):
        pl.semaphore_signal(barrier, inc=1, device_id={"tp": device}, device_id_type=MESH)
    own_copy = pltpu.make_async_copy(codes_hbm, rows_buf.at[rows_of(me), pl.ds(0, width)], load_sem.at[0])
    own_copy.start()
    gate_copy = pltpu.make_async_copy(gate_hbm, gate_buf, load_sem.at[1])
    gate_copy.start()
    up_copy = pltpu.make_async_copy(up_hbm, up_buf, load_sem.at[2])
    up_copy.start()
    row_id = lax.broadcasted_iota(jnp.int32, (SLOTS, SLOTS), 0)
    col_id = lax.broadcasted_iota(jnp.int32, (SLOTS, SLOTS), 1)
    kept = (row_id == col_id) & (row_id < counts_ref[0])
    spread = jnp.where(kept, scales_ref[...].astype(jnp.float32), 0.0)
    scale_col = jnp.sum(spread, axis=1, keepdims=True)
    rows_buf[rows_of(me), pl.ds(width, LANES)] = jnp.broadcast_to(scale_col, (SLOTS, LANES)).astype(jnp.bfloat16)
    own_copy.wait()
    pl.semaphore_wait(barrier, 3)

    def active(way, hop, s):
        return hop < far or (s < PIECES // 2) == (way == 0)

    def ring(way, hop, s, block):
        return pltpu.make_async_remote_copy(
            src_ref=rows_buf.at[rows_of(block), piece[s]],
            dst_ref=rows_buf.at[rows_of(block), piece[s]],
            send_sem=send_sem.at[way, hop - 1, s],
            recv_sem=recv_sem.at[way, hop - 1, s],
            device_id={"tp": at(signs[way])},
            device_id_type=MESH,
        )

    def share(way, hop, s, block):
        return pltpu.make_async_remote_copy(
            src_ref=rows_buf.at[rows_of(block), piece[s]],
            dst_ref=rows_buf.at[rows_of(block), piece[s]],
            send_sem=sib_send.at[way, hop, s],
            recv_sem=sib_recv.at[way, hop, s],
            device_id={"tp": sibling},
            device_id_type=MESH,
        )

    def project(distances):
        x = jnp.concatenate([rows_buf[chip_rows(d), pl.ds(0, width)] for d in distances], axis=0)
        scale = jnp.concatenate([rows_buf[chip_rows(d), pl.ds(width, LANES)] for d in distances], axis=0)
        scale = scale[:, 0:1].astype(jnp.float32)
        gate = jnp.dot(x, gate_buf[...], preferred_element_type=jnp.float32) * scale * gate_scales_ref[...]
        up = jnp.dot(x, up_buf[...], preferred_element_type=jnp.float32) * scale * up_scales_ref[...]
        hidden = (gate / (1.0 + jnp.exp(-gate)) * up).astype(jnp.bfloat16)
        peak = jnp.max(jnp.abs(hidden.astype(jnp.float32)), axis=1, keepdims=True)
        peak = jnp.broadcast_to(peak, (peak.shape[0], LANES))
        for i, d in enumerate(distances):
            part = slice(i * 2 * SLOTS, (i + 1) * 2 * SLOTS)
            hidden_ref[chip_rows(d), :] = hidden[part]
            local_peaks[chip_rows(d), :] = peak[part]

    def wait_shared(hop):
        for s in range(PIECES):
            for way in (0, 1):
                if active(way, hop, s) and not (hop == 0 and way == 1):
                    share(way, hop, s, me).wait_recv()

    for s in range(PIECES):
        for way in (0, 1):
            ring(way, 1, s, me).start()
    for s in range(PIECES):
        share(0, 0, s, me).start()
    for hop in range(1, far + 1):
        for s in range(PIECES):
            for way in (0, 1):
                if not active(way, hop, s):
                    continue
                block = at(-signs[way] * hop)
                ring(way, hop, s, block).wait_recv()
                if hop < far and active(way, hop + 1, s):
                    ring(way, hop + 1, s, block).start()
                share(way, hop, s, block).start()
        if hop == 2:
            gate_copy.wait()
            up_copy.wait()
            wait_shared(0)
            wait_shared(1)
            project((0, 1, -1))
        elif hop in (4, 6):
            wait_shared(hop - 2)
            wait_shared(hop - 1)
            project((hop - 2, 2 - hop, hop - 1, 1 - hop))
        elif hop == 7:
            wait_shared(6)
            project((6, -6))
    wait_shared(7)
    wait_shared(8)
    project((7, -7, 8))

    diagonal = lax.broadcasted_iota(jnp.int32, (LANES, LANES), 0) == lax.broadcasted_iota(jnp.int32, (LANES, LANES), 1)
    groups = row_count // LANES
    for g in range(groups):
        picked = jnp.where(diagonal, local_peaks[g * LANES:(g + 1) * LANES, :], 0.0)
        own_peaks[g:g + 1, :] = jnp.max(picked, axis=0, keepdims=True)

    def peak_copy(step):
        return pltpu.make_async_remote_copy(
            src_ref=own_peaks,
            dst_ref=all_peaks.at[step - 1],
            send_sem=peak_send.at[step - 1],
            recv_sem=peak_recv.at[step - 1],
            device_id={"tp": lax.rem(me + step, tp)},
            device_id_type=MESH,
        )

    order = sorted(range(1, tp), key=lambda step: -min(step, tp - step))
    for step in order:
        peak_copy(step).start()
    for hop in range(1, far + 1):
        for s in range(PIECES):
            for way in (0, 1):
                if active(way, hop, s):
                    ring(way, hop, s, me).wait_send()
                    share(way, hop, s, me).wait_send()
    for s in range(PIECES):
        share(0, 0, s, me).wait_send()
    for step in reversed(order):
        peak_copy(step).wait()
    peaks = jnp.maximum(jnp.max(all_peaks[...], axis=0), own_peaks[...])
    peaks_ref[...] = jnp.maximum(peaks, 1e-5)


def shards(token_codes, token_scales, live_counts, gate_codes, up_codes, gate_scales, up_scales):
    tp = lax.axis_size("tp")
    width = token_codes.shape[1]
    hidden_units = gate_codes.shape[1]
    row_count = tp * SLOTS
    groups = row_count // LANES
    whole = pl.BlockSpec(memory_space=pltpu.VMEM)
    hbm = pl.BlockSpec(memory_space=pl.ANY)
    far = tp // 4
    dma = pltpu.SemaphoreType.DMA
    hidden, peaks = pl.pallas_call(
        functools.partial(kernel, tp, width, hidden_units),
        out_shape=(
            jax.ShapeDtypeStruct((row_count, hidden_units), jnp.bfloat16),
            jax.ShapeDtypeStruct((groups, LANES), jnp.float32),
        ),
        in_specs=[hbm, whole, pl.BlockSpec(memory_space=pltpu.SMEM), hbm, hbm, whole, whole],
        out_specs=(whole, whole),
        scratch_shapes=[
            pltpu.VMEM((row_count, width + LANES), jnp.bfloat16),
            pltpu.VMEM((width, hidden_units), jnp.bfloat16),
            pltpu.VMEM((width, hidden_units), jnp.bfloat16),
            pltpu.VMEM((row_count, LANES), jnp.float32),
            pltpu.VMEM((groups, LANES), jnp.float32),
            pltpu.VMEM((tp - 1, groups, LANES), jnp.float32),
            dma((2, far, PIECES)),
            dma((2, far, PIECES)),
            dma((2, far + 1, PIECES)),
            dma((2, far + 1, PIECES)),
            dma((tp - 1,)),
            dma((tp - 1,)),
            dma((3,)),
        ],
        compiler_params=pltpu.CompilerParams(
            collective_id=0, has_side_effects=True, vmem_limit_bytes=40 << 20
        ),
    )(
        token_codes, token_scales[None, :], live_counts, gate_codes, up_codes,
        gate_scales[None, :], up_scales[None, :],
    )
    row_peak = peaks.reshape(row_count)
    down_input = (hidden.astype(jnp.float32) / row_peak[:, None]).astype(jnp.bfloat16)
    return (down_input, row_peak)


def solution(mesh):
    in_specs = (
        P(("dp", "tp"), None),
        P(("dp", "tp")),
        P(("dp", "tp")),
        P(None, "tp"),
        P(None, "tp"),
        P("tp"),
        P("tp"),
    )
    out_specs = (P("dp", "tp"), P("dp"))
    return jax.shard_map(shards, mesh=mesh, in_specs=in_specs, out_specs=out_specs, check_vma=False)
```

```python
import functools

import jax
import jax.numpy as jnp
from jax import lax
from jax.experimental import pallas as pl
from jax.experimental.pallas import tpu as pltpu
from jax.sharding import PartitionSpec as P

MESH = pl.DeviceIdType.MESH
SLOTS = 16
PIECES = 4
LANES = 128


def equal_ids(rows, columns):
    shape = (rows, columns)
    return lax.broadcasted_iota(jnp.int32, shape, 0) == lax.broadcasted_iota(jnp.int32, shape, 1)


def kernel(
    tp, width, units,
    codes_hbm, scales_ref, counts_ref, gate_hbm, up_hbm, gate_scales_ref, up_scales_ref,
    hidden_ref, peaks_ref,
    rows_buf, weights, channel_scales, own_peaks, all_peaks,
    send_sem, recv_sem, sib_send, sib_recv, peak_send, peak_recv, load_sem,
):
    me = lax.axis_index("tp")
    chips = tp // 2
    far = chips // 2
    sibling = me + 1 - 2 * lax.rem(me, 2)
    chip = me // 2
    groups = tp * SLOTS // LANES
    group_chips = chips // groups
    full = width + LANES

    def at(distance):
        return lax.rem(me + 2 * distance + 2 * tp, tp)

    def rows_of(device):
        return pl.ds(pl.multiple_of(device * SLOTS, SLOTS), SLOTS)

    tiles = full // LANES
    edges = [(tiles * s) // PIECES * LANES for s in range(PIECES + 1)]
    piece = [pl.ds(a, b - a) for a, b in zip(edges[:-1], edges[1:])]
    signs = (1, -1)

    barrier = pltpu.get_barrier_semaphore()
    for device in (at(1), at(-1), sibling):
        pl.semaphore_signal(barrier, inc=1, device_id={"tp": device}, device_id_type=MESH)
    own_copy = pltpu.make_async_copy(codes_hbm, rows_buf.at[rows_of(me), pl.ds(0, width)], load_sem.at[0])
    own_copy.start()
    gate_copy = pltpu.make_async_copy(gate_hbm, weights.at[pl.ds(0, units)], load_sem.at[1])
    gate_copy.start()
    up_copy = pltpu.make_async_copy(up_hbm, weights.at[pl.ds(units, units)], load_sem.at[2])
    up_copy.start()
    kept = equal_ids(SLOTS, SLOTS) & (lax.broadcasted_iota(jnp.int32, (SLOTS, SLOTS), 0) < counts_ref[0])
    spread = jnp.where(kept, scales_ref[...].astype(jnp.float32), 0.0)
    scale_col = jnp.sum(spread, axis=1, keepdims=True)
    rows_buf[rows_of(me), pl.ds(width, LANES)] = jnp.broadcast_to(scale_col, (SLOTS, LANES)).astype(jnp.bfloat16)
    own_copy.wait()
    pl.semaphore_wait(barrier, 3)

    def active(way, hop, s):
        return hop < far or (s < PIECES // 2) == (way == 0)

    def ring(way, hop, s, block):
        return pltpu.make_async_remote_copy(
            src_ref=rows_buf.at[rows_of(block), piece[s]],
            dst_ref=rows_buf.at[rows_of(block), piece[s]],
            send_sem=send_sem.at[way, hop - 1, s],
            recv_sem=recv_sem.at[way, hop - 1, s],
            device_id={"tp": at(signs[way])},
            device_id_type=MESH,
        )

    def share(way, hop, s, block):
        return pltpu.make_async_remote_copy(
            src_ref=rows_buf.at[rows_of(block), piece[s]],
            dst_ref=rows_buf.at[rows_of(block), piece[s]],
            send_sem=sib_send.at[way, hop, s],
            recv_sem=sib_recv.at[way, hop, s],
            device_id={"tp": sibling},
            device_id_type=MESH,
        )

    first = chip // group_chips
    nearer = 2 * (lax.rem(chip, group_chips) // (group_chips // 2)) - 1
    ranked = [lax.rem(first + groups + step, groups) for step in (0, nearer, -nearer, 2)]

    def project(picked):
        spans = [pl.ds(pl.multiple_of(ranked[i] * LANES, LANES), LANES) for i in picked]
        x = jnp.concatenate([rows_buf[span, pl.ds(0, width)] for span in spans], axis=0)
        values = lax.dot_general(
            weights[...], x, (((1,), (1,)), ((), ())), preferred_element_type=jnp.float32
        )
        for i, span in enumerate(spans):
            spread = jnp.where(equal_ids(LANES, LANES), rows_buf[span, pl.ds(width, LANES)].astype(jnp.float32), 0.0)
            scale = jnp.sum(spread, axis=0, keepdims=True)
            part = values[:, i * LANES:(i + 1) * LANES]
            gate = part[:units] * scale * channel_scales[:, 0:1]
            up = part[units:] * scale * channel_scales[:, 1:2]
            hidden = (gate / (1.0 + jnp.exp(-gate)) * up).astype(jnp.bfloat16)
            hidden_ref[:, span] = hidden
            peak = jnp.max(jnp.abs(hidden.astype(jnp.float32)), axis=0, keepdims=True)
            own_peaks[pl.ds(ranked[picked[i]], 1), :] = peak

    def wait_shared(hop):
        for s in range(PIECES):
            for way in (0, 1):
                if active(way, hop, s) and not (hop == 0 and way == 1):
                    share(way, hop, s, me).wait_recv()

    for s in range(PIECES):
        for way in (0, 1):
            ring(way, 1, s, me).start()
    for s in range(PIECES):
        share(0, 0, s, me).start()
    for hop in range(1, far + 1):
        for s in range(PIECES):
            for way in (0, 1):
                if not active(way, hop, s):
                    continue
                block = at(-signs[way] * hop)
                ring(way, hop, s, block).wait_recv()
                if hop < far and active(way, hop + 1, s):
                    ring(way, hop + 1, s, block).start()
                share(way, hop, s, block).start()
        if hop == 1:
            for k, ref in enumerate((gate_scales_ref, up_scales_ref)):
                spread = jnp.where(equal_ids(units, units), ref[...], 0.0)
                channel_scales[:, k:k + 1] = jnp.sum(spread, axis=1, keepdims=True)
        elif hop == 6:
            gate_copy.wait()
            up_copy.wait()
            for earlier in range(6):
                wait_shared(earlier)
            project((0, 1))
    for earlier in (6, 7, 8):
        wait_shared(earlier)
    project((2, 3))

    def peak_copy(step):
        return pltpu.make_async_remote_copy(
            src_ref=own_peaks,
            dst_ref=all_peaks.at[step - 1],
            send_sem=peak_send.at[step - 1],
            recv_sem=peak_recv.at[step - 1],
            device_id={"tp": lax.rem(me + step, tp)},
            device_id_type=MESH,
        )

    order = sorted(range(1, tp), key=lambda step: -min(step, tp - step))
    for step in order:
        peak_copy(step).start()
    for hop in range(1, far + 1):
        for s in range(PIECES):
            for way in (0, 1):
                if active(way, hop, s):
                    ring(way, hop, s, me).wait_send()
                    share(way, hop, s, me).wait_send()
    for s in range(PIECES):
        share(0, 0, s, me).wait_send()
    for step in reversed(order):
        peak_copy(step).wait()
    peaks = jnp.maximum(jnp.max(all_peaks[...], axis=0), own_peaks[...])
    peaks_ref[...] = jnp.maximum(peaks, 1e-5)


def shards(token_codes, token_scales, live_counts, gate_codes, up_codes, gate_scales, up_scales):
    tp = lax.axis_size("tp")
    width = token_codes.shape[1]
    units = gate_codes.shape[1]
    row_count = tp * SLOTS
    groups = row_count // LANES
    whole = pl.BlockSpec(memory_space=pltpu.VMEM)
    hbm = pl.BlockSpec(memory_space=pltpu.HBM)
    far = tp // 4
    dma = pltpu.SemaphoreType.DMA
    hidden, peaks = pl.pallas_call(
        functools.partial(kernel, tp, width, units),
        out_shape=(
            jax.ShapeDtypeStruct((units, row_count), jnp.bfloat16),
            jax.ShapeDtypeStruct((groups, LANES), jnp.float32),
        ),
        in_specs=[hbm, whole, pl.BlockSpec(memory_space=pltpu.SMEM), hbm, hbm, whole, whole],
        out_specs=(whole, whole),
        scratch_shapes=[
            pltpu.VMEM((row_count, width + LANES), jnp.bfloat16),
            pltpu.VMEM((2 * units, width), jnp.bfloat16),
            pltpu.VMEM((units, LANES), jnp.float32),
            pltpu.VMEM((groups, LANES), jnp.float32),
            pltpu.VMEM((tp - 1, groups, LANES), jnp.float32),
            dma((2, far, PIECES)),
            dma((2, far, PIECES)),
            dma((2, far + 1, PIECES)),
            dma((2, far + 1, PIECES)),
            dma((tp - 1,)),
            dma((tp - 1,)),
            dma((3,)),
        ],
        compiler_params=pltpu.CompilerParams(
            collective_id=0, has_side_effects=True, vmem_limit_bytes=60 << 20
        ),
    )(
        token_codes, token_scales[None, :], live_counts, gate_codes.T, up_codes.T,
        gate_scales[None, :], up_scales[None, :],
    )
    row_peak = peaks.reshape(row_count)
    down_input = (hidden.astype(jnp.float32) / row_peak[None, :]).astype(jnp.bfloat16)
    return (down_input.T, row_peak)


def solution(mesh):
    in_specs = (
        P(("dp", "tp"), None),
        P(("dp", "tp")),
        P(("dp", "tp")),
        P(None, "tp"),
        P(None, "tp"),
        P("tp"),
        P("tp"),
    )
    out_specs = (P("dp", "tp"), P("dp"))
    return jax.shard_map(shards, mesh=mesh, in_specs=in_specs, out_specs=out_specs, check_vma=False)
```

```python
import functools

import jax
import jax.numpy as jnp
from jax import lax
from jax.experimental import pallas as pl
from jax.experimental.pallas import tpu as pltpu
from jax.sharding import PartitionSpec as P

MESH = pl.DeviceIdType.MESH
SLOTS = 16
PIECES = 4
LANES = 128


def equal_ids(rows, columns):
    shape = (rows, columns)
    return lax.broadcasted_iota(jnp.int32, shape, 0) == lax.broadcasted_iota(jnp.int32, shape, 1)


def kernel(
    tp, width, units,
    codes_hbm, scales_ref, counts_ref, gate_hbm, up_hbm, gate_scales_ref, up_scales_ref,
    hidden_hbm, peaks_ref,
    hidden_buf, rows_buf, weights, early_gates, channel_scales, own_peaks, all_peaks,
    send_sem, recv_sem, sib_send, sib_recv, peak_send, peak_recv, load_sem,
):
    me = lax.axis_index("tp")
    chips = tp // 2
    far = chips // 2
    sibling = me + 1 - 2 * lax.rem(me, 2)
    chip = me // 2
    groups = tp * SLOTS // LANES
    group_chips = chips // groups
    full = width + LANES

    def at(distance):
        return lax.rem(me + 2 * distance + 2 * tp, tp)

    def rows_of(device):
        return pl.ds(pl.multiple_of(device * SLOTS, SLOTS), SLOTS)

    tiles = full // LANES
    edges = [(tiles * s) // PIECES * LANES for s in range(PIECES + 1)]
    piece = [pl.ds(a, b - a) for a, b in zip(edges[:-1], edges[1:])]
    signs = (1, -1)
    every = pl.ds(0, width)

    barrier = pltpu.get_barrier_semaphore()
    for device in (at(1), at(-1), sibling):
        pl.semaphore_signal(barrier, inc=1, device_id={"tp": device}, device_id_type=MESH)
    own_copy = pltpu.make_async_copy(codes_hbm, rows_buf.at[rows_of(me), pl.ds(0, width)], load_sem.at[0])
    own_copy.start()
    gate_copy = pltpu.make_async_copy(gate_hbm, weights.at[pl.ds(0, units)], load_sem.at[1])
    gate_copy.start()
    up_copy = pltpu.make_async_copy(up_hbm, weights.at[pl.ds(units, units)], load_sem.at[2])
    up_copy.start()
    kept = equal_ids(SLOTS, SLOTS) & (lax.broadcasted_iota(jnp.int32, (SLOTS, SLOTS), 0) < counts_ref[0])
    spread = jnp.where(kept, scales_ref[...].astype(jnp.float32), 0.0)
    scale_col = jnp.sum(spread, axis=1, keepdims=True)
    rows_buf[rows_of(me), pl.ds(width, LANES)] = jnp.broadcast_to(scale_col, (SLOTS, LANES)).astype(jnp.bfloat16)
    own_copy.wait()
    pl.semaphore_wait(barrier, 3)

    def active(way, hop, s):
        return hop < far or (s < PIECES // 2) == (way == 0)

    def ring(way, hop, s, block):
        return pltpu.make_async_remote_copy(
            src_ref=rows_buf.at[rows_of(block), piece[s]],
            dst_ref=rows_buf.at[rows_of(block), piece[s]],
            send_sem=send_sem.at[way, hop - 1, s],
            recv_sem=recv_sem.at[way, hop - 1, s],
            device_id={"tp": at(signs[way])},
            device_id_type=MESH,
        )

    def share(way, hop, s, block):
        return pltpu.make_async_remote_copy(
            src_ref=rows_buf.at[rows_of(block), piece[s]],
            dst_ref=rows_buf.at[rows_of(block), piece[s]],
            send_sem=sib_send.at[way, hop, s],
            recv_sem=sib_recv.at[way, hop, s],
            device_id={"tp": sibling},
            device_id_type=MESH,
        )

    first = chip // group_chips
    nearer = 2 * (lax.rem(chip, group_chips) // (group_chips // 2)) - 1
    ranked = [lax.rem(first + groups + step, groups) for step in (0, nearer, -nearer, 2)]

    def spans_of(picked):
        return [pl.ds(pl.multiple_of(ranked[i] * LANES, LANES), LANES) for i in picked]

    def out_copy(i):
        span = spans_of((i,))[0]
        return pltpu.make_async_copy(hidden_buf.at[:, span], hidden_hbm.at[:, span], load_sem.at[3 + i])

    def multiply(picked, part, depth):
        x = jnp.concatenate([rows_buf[span, depth] for span in spans_of(picked)], axis=0)
        return lax.dot_general(
            weights[pl.ds(part * units, units), depth], x, (((1,), (1,)), ((), ())),
            preferred_element_type=jnp.float32,
        )

    def finish(picked, gates, ups):
        for i, span in enumerate(spans_of(picked)):
            spread = jnp.where(equal_ids(LANES, LANES), rows_buf[span, pl.ds(width, LANES)].astype(jnp.float32), 0.0)
            scale = jnp.sum(spread, axis=0, keepdims=True)
            lanes = slice(i * LANES, (i + 1) * LANES)
            gate = gates[:, lanes] * scale * channel_scales[:, 0:1]
            up = ups[:, lanes] * scale * channel_scales[:, 1:2]
            hidden = (gate / (1.0 + jnp.exp(-gate)) * up).astype(jnp.bfloat16)
            hidden_buf[:, span] = hidden
            out_copy(picked[i]).start()
            peak = jnp.max(jnp.abs(hidden.astype(jnp.float32)), axis=0, keepdims=True)
            own_peaks[pl.ds(ranked[picked[i]], 1), :] = peak

    def wait_shared(hop):
        for s in range(PIECES):
            for way in (0, 1):
                if active(way, hop, s) and not (hop == 0 and way == 1):
                    share(way, hop, s, me).wait_recv()

    for s in range(PIECES):
        for way in (0, 1):
            ring(way, 1, s, me).start()
    for s in range(PIECES):
        share(0, 0, s, me).start()
    for hop in range(1, far + 1):
        for s in range(PIECES):
            for way in (0, 1):
                if not active(way, hop, s):
                    continue
                block = at(-signs[way] * hop)
                ring(way, hop, s, block).wait_recv()
                if hop < far and active(way, hop + 1, s):
                    ring(way, hop + 1, s, block).start()
                share(way, hop, s, block).start()
        if hop == 1:
            for k, ref in enumerate((gate_scales_ref, up_scales_ref)):
                spread = jnp.where(equal_ids(units, units), ref[...].reshape(1, units), 0.0)
                channel_scales[:, k:k + 1] = jnp.sum(spread, axis=1, keepdims=True)
        elif hop == 6:
            gate_copy.wait()
            up_copy.wait()
            for earlier in range(6):
                wait_shared(earlier)
            early_gates[...] = multiply((0, 1), 0, every)
        elif hop == 7:
            finish((0, 1), early_gates[...], multiply((0, 1), 1, every))
            wait_shared(6)
            wait_shared(7)
            finish((2,), multiply((2,), 0, every), multiply((2,), 1, every))
    wait_shared(8)
    finish((3,), multiply((3,), 0, every), multiply((3,), 1, every))

    def peak_copy(step):
        return pltpu.make_async_remote_copy(
            src_ref=own_peaks,
            dst_ref=all_peaks.at[step - 1],
            send_sem=peak_send.at[step - 1],
            recv_sem=peak_recv.at[step - 1],
            device_id={"tp": lax.rem(me + step, tp)},
            device_id_type=MESH,
        )

    order = sorted(range(1, tp), key=lambda step: -min(step, tp - step))
    for step in order:
        peak_copy(step).start()
    for hop in range(1, far + 1):
        for s in range(PIECES):
            for way in (0, 1):
                if active(way, hop, s):
                    ring(way, hop, s, me).wait_send()
                    share(way, hop, s, me).wait_send()
    for s in range(PIECES):
        share(0, 0, s, me).wait_send()
    for i in range(groups):
        out_copy(i).wait()
    for step in reversed(order):
        peak_copy(step).wait()
    peaks = jnp.maximum(jnp.max(all_peaks[...], axis=0), own_peaks[...])
    peaks_ref[...] = jnp.maximum(peaks, 1e-5)


def normalise(hidden_ref, peaks_ref, down_ref, row_peak_ref):
    for g in range(peaks_ref.shape[0]):
        span = slice(g * LANES, (g + 1) * LANES)
        peak = peaks_ref[g:g + 1, :]
        down_ref[:, span] = (hidden_ref[:, span].astype(jnp.float32) / peak).astype(jnp.bfloat16)
        row_peak_ref[span] = peak.reshape(LANES)


def shards(token_codes, token_scales, live_counts, gate_codes, up_codes, gate_scales, up_scales):
    tp = lax.axis_size("tp")
    width = token_codes.shape[1]
    units = gate_codes.shape[1]
    row_count = tp * SLOTS
    groups = row_count // LANES
    whole = pl.BlockSpec(memory_space=pltpu.VMEM)
    hbm = pl.BlockSpec(memory_space=pltpu.HBM)
    far = tp // 4
    dma = pltpu.SemaphoreType.DMA
    hidden, peaks = pl.pallas_call(
        functools.partial(kernel, tp, width, units),
        out_shape=(
            jax.ShapeDtypeStruct((units, row_count), jnp.bfloat16),
            jax.ShapeDtypeStruct((groups, LANES), jnp.float32),
        ),
        in_specs=[hbm, whole, pl.BlockSpec(memory_space=pltpu.SMEM), hbm, hbm, whole, whole],
        out_specs=(hbm, whole),
        scratch_shapes=[
            pltpu.VMEM((units, row_count), jnp.bfloat16),
            pltpu.VMEM((row_count, width + LANES), jnp.bfloat16),
            pltpu.VMEM((2 * units, width), jnp.bfloat16),
            pltpu.VMEM((units, 2 * LANES), jnp.float32),
            pltpu.VMEM((units, LANES), jnp.float32),
            pltpu.VMEM((groups, LANES), jnp.float32),
            pltpu.VMEM((tp - 1, groups, LANES), jnp.float32),
            dma((2, far, PIECES)),
            dma((2, far, PIECES)),
            dma((2, far + 1, PIECES)),
            dma((2, far + 1, PIECES)),
            dma((tp - 1,)),
            dma((tp - 1,)),
            dma((3 + groups,)),
        ],
        compiler_params=pltpu.CompilerParams(
            collective_id=0, has_side_effects=True, vmem_limit_bytes=60 << 20
        ),
    )(
        token_codes, token_scales[None, :], live_counts, gate_codes.T, up_codes.T,
        gate_scales, up_scales,
    )
    down_input, row_peak = pl.pallas_call(
        normalise,
        out_shape=(
            jax.ShapeDtypeStruct((units, row_count), jnp.bfloat16),
            jax.ShapeDtypeStruct((row_count,), jnp.float32),
        ),
        in_specs=[whole, whole],
        out_specs=(whole, whole),
    )(hidden, peaks)
    return (down_input.T, row_peak)


def solution(mesh):
    in_specs = (
        P(("dp", "tp"), None),
        P(("dp", "tp")),
        P(("dp", "tp")),
        P(None, "tp"),
        P(None, "tp"),
        P("tp"),
        P("tp"),
    )
    out_specs = (P("dp", "tp"), P("dp"))
    return jax.shard_map(shards, mesh=mesh, in_specs=in_specs, out_specs=out_specs, check_vma=False)
```

```python
import functools

import jax
import jax.numpy as jnp
from jax import lax
from jax.experimental import pallas as pl
from jax.experimental.pallas import tpu as pltpu
from jax.sharding import PartitionSpec as P

MESH = pl.DeviceIdType.MESH
SLOTS = 16
PIECES = 6
LANES = 128
EXTRA = 2 * LANES


def equal_ids(rows, columns):
    shape = (rows, columns)
    return lax.broadcasted_iota(jnp.int32, shape, 0) == lax.broadcasted_iota(jnp.int32, shape, 1)


def kernel(
    tp, width, units,
    codes_hbm, scales_ref, counts_ref, gate_hbm, up_hbm, gate_scales_ref, up_scales_ref,
    hidden_hbm, peaks_ref,
    hidden_buf, rows_buf, weights, early_gates, channel_scales, own_peaks, all_peaks,
    send_sem, recv_sem, sib_send, sib_recv, peak_send, peak_recv, load_sem,
):
    me = lax.axis_index("tp")
    chips = tp // 2
    far = chips // 2
    core = lax.rem(me, 2)
    sibling = me + 1 - 2 * core
    chip = me // 2
    groups = tp * SLOTS // LANES
    group_chips = chips // groups
    full = width + EXTRA
    every = pl.ds(0, width)

    toward = 1 - 2 * core
    ahead = lax.rem(me + 2 * toward + tp, tp)
    behind = lax.rem(me - 2 * toward + tp, tp)
    across = lax.rem(sibling - 2 * toward + tp, tp)

    def rows_of(device):
        return pl.ds(pl.multiple_of(device * SLOTS, SLOTS), SLOTS)

    def block(hop):
        start = lax.rem(chip - toward * hop + chips, chips) * (2 * SLOTS)
        return pl.ds(pl.multiple_of(start, 2 * SLOTS), 2 * SLOTS)

    def piece(s, server):
        index = lax.rem(s + server * (PIECES // 2), PIECES)
        return pl.ds(pl.multiple_of(index * (full // PIECES), LANES), full // PIECES)

    barrier = pltpu.get_barrier_semaphore()
    for device in (behind, across, sibling):
        pl.semaphore_signal(barrier, inc=1, device_id={"tp": device}, device_id_type=MESH)
    own_copy = pltpu.make_async_copy(codes_hbm, rows_buf.at[rows_of(me), every], load_sem.at[0])
    own_copy.start()
    gate_copy = pltpu.make_async_copy(gate_hbm, weights.at[pl.ds(0, units)], load_sem.at[1])
    gate_copy.start()
    up_copy = pltpu.make_async_copy(up_hbm, weights.at[pl.ds(units, units)], load_sem.at[2])
    up_copy.start()
    kept = equal_ids(SLOTS, SLOTS) & (lax.broadcasted_iota(jnp.int32, (SLOTS, SLOTS), 0) < counts_ref[0])
    spread = jnp.where(kept, scales_ref[...].astype(jnp.float32), 0.0)
    scale_col = jnp.sum(spread, axis=1, keepdims=True)
    rows_buf[rows_of(me), pl.ds(width, EXTRA)] = jnp.broadcast_to(scale_col, (SLOTS, EXTRA)).astype(jnp.bfloat16)
    own_copy.wait()
    pl.semaphore_wait(barrier, 3)

    def remote(span, columns, send, recv, device):
        part = rows_buf.at[span, columns]
        return pltpu.make_async_remote_copy(
            src_ref=part, dst_ref=part, send_sem=send, recv_sem=recv,
            device_id={"tp": device}, device_id_type=MESH,
        )

    def ring(hop, s):
        return remote(block(hop - 1), piece(s, core), send_sem.at[hop, s], recv_sem.at[hop, s], ahead)

    def own(way, s):
        server = core if way == 0 else 1 - core
        device = ahead if way == 0 else across
        return remote(rows_of(me), piece(s, server), send_sem.at[way, s], recv_sem.at[way, s], device)

    def share(hop, s):
        return remote(block(hop), piece(s, core), sib_send.at[hop, s], sib_recv.at[hop, s], sibling)

    own_share = remote(rows_of(me), pl.ds(0, full), sib_send.at[0, 0], sib_recv.at[0, 0], sibling)

    def pieces_at(hop):
        return PIECES if hop < far else PIECES // 2

    def wait_shared(hop):
        if hop == 0:
            own_share.wait_recv()
        else:
            for s in range(pieces_at(hop)):
                share(hop, s).wait_recv()

    first = chip // group_chips
    nearer = 2 * (lax.rem(chip, group_chips) // (group_chips // 2)) - 1
    ranked = [lax.rem(first + groups + step, groups) for step in (0, nearer, -nearer, 2)]

    def spans_of(picked):
        return [pl.ds(pl.multiple_of(ranked[i] * LANES, LANES), LANES) for i in picked]

    def out_copy(i):
        span = spans_of((i,))[0]
        return pltpu.make_async_copy(hidden_buf.at[:, span], hidden_hbm.at[:, span], load_sem.at[3 + i])

    def multiply(picked, part, depth):
        x = jnp.concatenate([rows_buf[span, depth] for span in spans_of(picked)], axis=0)
        return lax.dot_general(
            weights[pl.ds(part * units, units), depth], x, (((1,), (1,)), ((), ())),
            preferred_element_type=jnp.float32,
        )

    def finish(picked, gates, ups):
        for i, span in enumerate(spans_of(picked)):
            spread = jnp.where(equal_ids(LANES, LANES), rows_buf[span, pl.ds(width, LANES)].astype(jnp.float32), 0.0)
            scale = jnp.sum(spread, axis=0, keepdims=True)
            lanes = slice(i * LANES, (i + 1) * LANES)
            gate = gates[:, lanes] * scale * channel_scales[:, 0:1]
            up = ups[:, lanes] * scale * channel_scales[:, 1:2]
            hidden = (gate / (1.0 + jnp.exp(-gate)) * up).astype(jnp.bfloat16)
            hidden_buf[:, span] = hidden
            out_copy(picked[i]).start()
            peak = jnp.max(jnp.abs(hidden.astype(jnp.float32)), axis=0, keepdims=True)
            own_peaks[pl.ds(ranked[picked[i]], 1), :] = peak

    for s in range(PIECES):
        own(0, s).start()
        own(1, s).start()
    own_share.start()
    for hop in range(1, far + 1):
        for s in range(pieces_at(hop)):
            if hop == 1:
                own(0, s).wait_recv()
                own(1, s).wait_recv()
            else:
                ring(hop, s).wait_recv()
            if hop < far and s < pieces_at(hop + 1):
                ring(hop + 1, s).start()
            share(hop, s).start()
        if hop == 1:
            for k, ref in enumerate((gate_scales_ref, up_scales_ref)):
                spread = jnp.where(equal_ids(units, units), ref[...].reshape(1, units), 0.0)
                channel_scales[:, k:k + 1] = jnp.sum(spread, axis=1, keepdims=True)
        elif hop == 6:
            gate_copy.wait()
            up_copy.wait()
            for earlier in range(6):
                wait_shared(earlier)
            early_gates[...] = multiply((0, 1), 0, every)
        elif hop == 7:
            finish((0, 1), early_gates[...], multiply((0, 1), 1, every))
            wait_shared(6)
            wait_shared(7)
            finish((2,), multiply((2,), 0, every), multiply((2,), 1, every))
    wait_shared(8)
    finish((3,), multiply((3,), 0, every), multiply((3,), 1, every))

    def peak_copy(step):
        return pltpu.make_async_remote_copy(
            src_ref=own_peaks,
            dst_ref=all_peaks.at[step - 1],
            send_sem=peak_send.at[step - 1],
            recv_sem=peak_recv.at[step - 1],
            device_id={"tp": lax.rem(me + step, tp)},
            device_id_type=MESH,
        )

    order = sorted(range(1, tp), key=lambda step: -min(step, tp - step))
    for step in order:
        peak_copy(step).start()
    own_share.wait_send()
    for hop in range(1, far + 1):
        for s in range(pieces_at(hop)):
            if hop == 1:
                own(0, s).wait_send()
                own(1, s).wait_send()
            else:
                ring(hop, s).wait_send()
            share(hop, s).wait_send()
    for i in range(groups):
        out_copy(i).wait()
    for step in reversed(order):
        peak_copy(step).wait()
    peaks = jnp.maximum(jnp.max(all_peaks[...], axis=0), own_peaks[...])
    peaks_ref[...] = jnp.maximum(peaks, 1e-5)


def normalise(hidden_ref, peaks_ref, down_ref, row_peak_ref):
    for g in range(peaks_ref.shape[0]):
        span = slice(g * LANES, (g + 1) * LANES)
        peak = peaks_ref[g:g + 1, :]
        down_ref[:, span] = (hidden_ref[:, span].astype(jnp.float32) / peak).astype(jnp.bfloat16)
        row_peak_ref[span] = peak.reshape(LANES)


def shards(token_codes, token_scales, live_counts, gate_codes, up_codes, gate_scales, up_scales):
    tp = lax.axis_size("tp")
    width = token_codes.shape[1]
    units = gate_codes.shape[1]
    row_count = tp * SLOTS
    groups = row_count // LANES
    whole = pl.BlockSpec(memory_space=pltpu.VMEM)
    hbm = pl.BlockSpec(memory_space=pltpu.HBM)
    far = tp // 4
    dma = pltpu.SemaphoreType.DMA
    hidden, peaks = pl.pallas_call(
        functools.partial(kernel, tp, width, units),
        out_shape=(
            jax.ShapeDtypeStruct((units, row_count), jnp.bfloat16),
            jax.ShapeDtypeStruct((groups, LANES), jnp.float32),
        ),
        in_specs=[hbm, whole, pl.BlockSpec(memory_space=pltpu.SMEM), hbm, hbm, whole, whole],
        out_specs=(hbm, whole),
        scratch_shapes=[
            pltpu.VMEM((units, row_count), jnp.bfloat16),
            pltpu.VMEM((row_count, width + EXTRA), jnp.bfloat16),
            pltpu.VMEM((2 * units, width), jnp.bfloat16),
            pltpu.VMEM((units, 2 * LANES), jnp.float32),
            pltpu.VMEM((units, LANES), jnp.float32),
            pltpu.VMEM((groups, LANES), jnp.float32),
            pltpu.VMEM((tp - 1, groups, LANES), jnp.float32),
            dma((far + 1, PIECES)),
            dma((far + 1, PIECES)),
            dma((far + 1, PIECES)),
            dma((far + 1, PIECES)),
            dma((tp - 1,)),
            dma((tp - 1,)),
            dma((3 + groups,)),
        ],
        compiler_params=pltpu.CompilerParams(
            collective_id=0, has_side_effects=True, vmem_limit_bytes=60 << 20
        ),
    )(
        token_codes, token_scales[None, :], live_counts, gate_codes.T, up_codes.T,
        gate_scales, up_scales,
    )
    down_input, row_peak = pl.pallas_call(
        normalise,
        out_shape=(
            jax.ShapeDtypeStruct((units, row_count), jnp.bfloat16),
            jax.ShapeDtypeStruct((row_count,), jnp.float32),
        ),
        in_specs=[whole, whole],
        out_specs=(whole, whole),
    )(hidden, peaks)
    return (down_input.T, row_peak)


def solution(mesh):
    in_specs = (
        P(("dp", "tp"), None),
        P(("dp", "tp")),
        P(("dp", "tp")),
        P(None, "tp"),
        P(None, "tp"),
        P("tp"),
        P("tp"),
    )
    out_specs = (P("dp", "tp"), P("dp"))
    return jax.shard_map(shards, mesh=mesh, in_specs=in_specs, out_specs=out_specs, check_vma=False)
```

```python
import functools

import jax
import jax.numpy as jnp
from jax import lax
from jax.experimental import pallas as pl
from jax.experimental.pallas import tpu as pltpu
from jax.sharding import PartitionSpec as P

MESH = pl.DeviceIdType.MESH
SLOTS = 16
PIECES = 6
LANES = 128
EXTRA = 2 * LANES


def equal_ids(rows, columns):
    shape = (rows, columns)
    return lax.broadcasted_iota(jnp.int32, shape, 0) == lax.broadcasted_iota(jnp.int32, shape, 1)


def kernel(
    tp, width, units,
    codes_hbm, scales_hbm, counts_hbm, gate_hbm, up_hbm, gate_scales_hbm, up_scales_hbm,
    hidden_hbm, peaks_ref,
    hidden_buf, rows_buf, weights, early_gates, channel_scales, own_peaks, all_peaks,
    scales_ref, counts_ref, gate_scales_ref, up_scales_ref,
    send_sem, recv_sem, sib_send, sib_recv, peak_send, peak_recv, load_sem,
):
    me = lax.axis_index("tp")
    chips = tp // 2
    far = chips // 2
    core = lax.rem(me, 2)
    sibling = me + 1 - 2 * core
    chip = me // 2
    groups = tp * SLOTS // LANES
    group_chips = chips // groups
    full = width + EXTRA
    every = pl.ds(0, width)

    toward = 1 - 2 * core
    ahead = lax.rem(me + 2 * toward + tp, tp)
    behind = lax.rem(me - 2 * toward + tp, tp)
    across = lax.rem(sibling - 2 * toward + tp, tp)

    def rows_of(device):
        return pl.ds(pl.multiple_of(device * SLOTS, SLOTS), SLOTS)

    def block(hop):
        start = lax.rem(chip - toward * hop + chips, chips) * (2 * SLOTS)
        return pl.ds(pl.multiple_of(start, 2 * SLOTS), 2 * SLOTS)

    def piece(s, server):
        index = lax.rem(s + server * (PIECES // 2), PIECES)
        return pl.ds(pl.multiple_of(index * (full // PIECES), LANES), full // PIECES)

    barrier = pltpu.get_barrier_semaphore()
    for device in (behind, across, sibling):
        pl.semaphore_signal(barrier, inc=1, device_id={"tp": device}, device_id_type=MESH)
    own_copy = pltpu.make_async_copy(codes_hbm, rows_buf.at[rows_of(me), every], load_sem.at[0])
    own_copy.start()
    small_copies = [
        pltpu.make_async_copy(source, target, load_sem.at[3 + groups + i])
        for i, (source, target) in enumerate((
            (scales_hbm, scales_ref), (counts_hbm, counts_ref),
            (gate_scales_hbm, gate_scales_ref), (up_scales_hbm, up_scales_ref),
        ))
    ]
    for copy in small_copies:
        copy.start()
    gate_copy = pltpu.make_async_copy(gate_hbm, weights.at[pl.ds(0, units)], load_sem.at[1])
    gate_copy.start()
    up_copy = pltpu.make_async_copy(up_hbm, weights.at[pl.ds(units, units)], load_sem.at[2])
    up_copy.start()
    small_copies[0].wait()
    small_copies[1].wait()
    kept = equal_ids(SLOTS, SLOTS) & (lax.broadcasted_iota(jnp.int32, (SLOTS, SLOTS), 0) < counts_ref[0])
    spread = jnp.where(kept, scales_ref[...].astype(jnp.float32), 0.0)
    scale_col = jnp.sum(spread, axis=1, keepdims=True)
    rows_buf[rows_of(me), pl.ds(width, EXTRA)] = jnp.broadcast_to(scale_col, (SLOTS, EXTRA)).astype(jnp.bfloat16)
    own_copy.wait()
    pl.semaphore_wait(barrier, 3)

    def remote(span, columns, send, recv, device):
        part = rows_buf.at[span, columns]
        return pltpu.make_async_remote_copy(
            src_ref=part, dst_ref=part, send_sem=send, recv_sem=recv,
            device_id={"tp": device}, device_id_type=MESH,
        )

    def ring(hop, s):
        return remote(block(hop - 1), piece(s, core), send_sem.at[hop, s], recv_sem.at[hop, s], ahead)

    def own(way, s):
        server = core if way == 0 else 1 - core
        device = ahead if way == 0 else across
        return remote(rows_of(me), piece(s, server), send_sem.at[way, s], recv_sem.at[way, s], device)

    def share(hop, s):
        columns = pl.ds(0, full) if hop < far else piece(s, core)
        return remote(block(hop), columns, sib_send.at[hop, s], sib_recv.at[hop, s], sibling)

    def shares_at(hop):
        return 1 if hop < far else PIECES // 2

    own_share = remote(rows_of(me), pl.ds(0, full), sib_send.at[0, 0], sib_recv.at[0, 0], sibling)

    def pieces_at(hop):
        return PIECES if hop < far else PIECES // 2

    def wait_shared(hop):
        if hop == 0:
            own_share.wait_recv()
        else:
            for s in range(shares_at(hop)):
                share(hop, s).wait_recv()

    first = chip // group_chips
    nearer = 2 * (lax.rem(chip, group_chips) // (group_chips // 2)) - 1
    ranked = [lax.rem(first + groups + step, groups) for step in (0, nearer, -nearer, 2)]

    def spans_of(picked):
        return [pl.ds(pl.multiple_of(ranked[i] * LANES, LANES), LANES) for i in picked]

    def out_copy(i):
        span = spans_of((i,))[0]
        return pltpu.make_async_copy(hidden_buf.at[:, span], hidden_hbm.at[:, span], load_sem.at[3 + i])

    def multiply(picked, part, depth):
        x = jnp.concatenate([rows_buf[span, depth] for span in spans_of(picked)], axis=0)
        return lax.dot_general(
            weights[pl.ds(part * units, units), depth], x, (((1,), (1,)), ((), ())),
            preferred_element_type=jnp.float32,
        )

    def finish(picked, gates, ups):
        for i, span in enumerate(spans_of(picked)):
            spread = jnp.where(equal_ids(LANES, LANES), rows_buf[span, pl.ds(width, LANES)].astype(jnp.float32), 0.0)
            scale = jnp.sum(spread, axis=0, keepdims=True)
            lanes = slice(i * LANES, (i + 1) * LANES)
            gate = gates[:, lanes] * scale * channel_scales[:, 0:1]
            up = ups[:, lanes] * scale * channel_scales[:, 1:2]
            hidden = (gate / (1.0 + jnp.exp(-gate)) * up).astype(jnp.bfloat16)
            hidden_buf[:, span] = hidden
            out_copy(picked[i]).start()
            peak = jnp.max(jnp.abs(hidden.astype(jnp.float32)), axis=0, keepdims=True)
            own_peaks[pl.ds(ranked[picked[i]], 1), :] = peak

    for s in range(PIECES):
        own(0, s).start()
        own(1, s).start()
    own_share.start()
    for hop in range(1, far + 1):
        for s in range(pieces_at(hop)):
            if hop == 1:
                own(0, s).wait_recv()
                own(1, s).wait_recv()
            else:
                ring(hop, s).wait_recv()
            if hop < far and s < pieces_at(hop + 1):
                ring(hop + 1, s).start()
            if hop == far or s == PIECES - 1:
                share(hop, 0 if hop < far else s).start()
        if hop == 1:
            small_copies[2].wait()
            small_copies[3].wait()
            for k, ref in enumerate((gate_scales_ref, up_scales_ref)):
                spread = jnp.where(equal_ids(units, units), ref[...].reshape(1, units), 0.0)
                channel_scales[:, k:k + 1] = jnp.sum(spread, axis=1, keepdims=True)
        elif hop == 6:
            gate_copy.wait()
            up_copy.wait()
            for earlier in range(6):
                wait_shared(earlier)
            early_gates[...] = multiply((0, 1), 0, every)
        elif hop == 7:
            finish((0, 1), early_gates[...], multiply((0, 1), 1, every))
    for earlier in (6, 7, 8):
        wait_shared(earlier)
    finish((2, 3), multiply((2, 3), 0, every), multiply((2, 3), 1, every))

    def peak_copy(step):
        return pltpu.make_async_remote_copy(
            src_ref=own_peaks,
            dst_ref=all_peaks.at[step - 1],
            send_sem=peak_send.at[step - 1],
            recv_sem=peak_recv.at[step - 1],
            device_id={"tp": lax.rem(me + step, tp)},
            device_id_type=MESH,
        )

    order = sorted(range(1, tp), key=lambda step: -min(step, tp - step))
    for step in order:
        peak_copy(step).start()
    own_share.wait_send()
    for hop in range(1, far + 1):
        for s in range(pieces_at(hop)):
            if hop == 1:
                own(0, s).wait_send()
                own(1, s).wait_send()
            else:
                ring(hop, s).wait_send()
        for s in range(shares_at(hop)):
            share(hop, s).wait_send()
    for i in range(groups):
        out_copy(i).wait()
    for step in reversed(order):
        peak_copy(step).wait()
    peaks = jnp.maximum(jnp.max(all_peaks[...], axis=0), own_peaks[...])
    peaks_ref[...] = jnp.maximum(peaks, 1e-5)


def normalise(hidden_ref, peaks_ref, down_ref, row_peak_ref):
    for g in range(peaks_ref.shape[0]):
        span = slice(g * LANES, (g + 1) * LANES)
        peak = peaks_ref[g:g + 1, :]
        down_ref[:, span] = (hidden_ref[:, span].astype(jnp.float32) / peak).astype(jnp.bfloat16)
        row_peak_ref[span] = peak.reshape(LANES)


def shards(token_codes, token_scales, live_counts, gate_codes, up_codes, gate_scales, up_scales):
    tp = lax.axis_size("tp")
    width = token_codes.shape[1]
    units = gate_codes.shape[1]
    row_count = tp * SLOTS
    groups = row_count // LANES
    whole = pl.BlockSpec(memory_space=pltpu.VMEM)
    hbm = pl.BlockSpec(memory_space=pltpu.HBM)
    far = tp // 4
    dma = pltpu.SemaphoreType.DMA
    hidden, peaks = pl.pallas_call(
        functools.partial(kernel, tp, width, units),
        out_shape=(
            jax.ShapeDtypeStruct((units, row_count), jnp.bfloat16),
            jax.ShapeDtypeStruct((groups, LANES), jnp.float32),
        ),
        in_specs=[hbm] * 7,
        out_specs=(hbm, whole),
        scratch_shapes=[
            pltpu.VMEM((units, row_count), jnp.bfloat16),
            pltpu.VMEM((row_count, width + EXTRA), jnp.bfloat16),
            pltpu.VMEM((2 * units, width), jnp.bfloat16),
            pltpu.VMEM((units, 2 * LANES), jnp.float32),
            pltpu.VMEM((units, LANES), jnp.float32),
            pltpu.VMEM((groups, LANES), jnp.float32),
            pltpu.VMEM((tp - 1, groups, LANES), jnp.float32),
            pltpu.VMEM((1, SLOTS), jnp.bfloat16),
            pltpu.SMEM((1,), jnp.int32),
            pltpu.VMEM((units,), jnp.float32),
            pltpu.VMEM((units,), jnp.float32),
            dma((far + 1, PIECES)),
            dma((far + 1, PIECES)),
            dma((far + 1, PIECES)),
            dma((far + 1, PIECES)),
            dma((tp - 1,)),
            dma((tp - 1,)),
            dma((7 + groups,)),
        ],
        compiler_params=pltpu.CompilerParams(
            collective_id=0, has_side_effects=True, vmem_limit_bytes=60 << 20
        ),
    )(
        token_codes, token_scales[None, :], live_counts, gate_codes.T, up_codes.T,
        gate_scales, up_scales,
    )
    down_input, row_peak = pl.pallas_call(
        normalise,
        out_shape=(
            jax.ShapeDtypeStruct((units, row_count), jnp.bfloat16),
            jax.ShapeDtypeStruct((row_count,), jnp.float32),
        ),
        in_specs=[whole, whole],
        out_specs=(whole, whole),
    )(hidden, peaks)
    return (down_input.T, row_peak)


def solution(mesh):
    in_specs = (
        P(("dp", "tp"), None),
        P(("dp", "tp")),
        P(("dp", "tp")),
        P(None, "tp"),
        P(None, "tp"),
        P("tp"),
        P("tp"),
    )
    out_specs = (P("dp", "tp"), P("dp"))
    return jax.shard_map(shards, mesh=mesh, in_specs=in_specs, out_specs=out_specs, check_vma=False)
```

```python
import functools

import jax
import jax.numpy as jnp
from jax import lax
from jax.experimental import pallas as pl
from jax.experimental.pallas import tpu as pltpu
from jax.sharding import PartitionSpec as P

MESH = pl.DeviceIdType.MESH
SLOTS = 16
PIECES = 6
LANES = 128
EXTRA = 2 * LANES


def equal_ids(rows, columns):
    shape = (rows, columns)
    return lax.broadcasted_iota(jnp.int32, shape, 0) == lax.broadcasted_iota(jnp.int32, shape, 1)


def kernel(
    tp, width, units,
    codes_hbm, scales_hbm, counts_hbm, gate_hbm, up_hbm, gate_scales_hbm, up_scales_hbm,
    hidden_hbm, peaks_ref,
    hidden_buf, rows_buf, weights, early_gates, channel_scales, own_peaks, all_peaks, sibling_peaks,
    scales_ref, counts_ref, gate_scales_ref, up_scales_ref,
    send_sem, recv_sem, sib_send, sib_recv, peak_send, peak_recv, early_send, early_recv, load_sem,
):
    me = lax.axis_index("tp")
    chips = tp // 2
    far = chips // 2
    core = lax.rem(me, 2)
    sibling = me + 1 - 2 * core
    chip = me // 2
    groups = tp * SLOTS // LANES
    group_chips = chips // groups
    full = width + EXTRA
    every = pl.ds(0, width)

    toward = 1 - 2 * core
    ahead = lax.rem(me + 2 * toward + tp, tp)
    behind = lax.rem(me - 2 * toward + tp, tp)
    across = lax.rem(sibling - 2 * toward + tp, tp)

    def rows_of(device):
        return pl.ds(pl.multiple_of(device * SLOTS, SLOTS), SLOTS)

    def block(hop):
        start = lax.rem(chip - toward * hop + chips, chips) * (2 * SLOTS)
        return pl.ds(pl.multiple_of(start, 2 * SLOTS), 2 * SLOTS)

    def piece(s, server):
        index = lax.rem(s + server * (PIECES // 2), PIECES)
        return pl.ds(pl.multiple_of(index * (full // PIECES), LANES), full // PIECES)

    barrier = pltpu.get_barrier_semaphore()
    for device in (behind, across, sibling):
        pl.semaphore_signal(barrier, inc=1, device_id={"tp": device}, device_id_type=MESH)
    own_copy = pltpu.make_async_copy(codes_hbm, rows_buf.at[rows_of(me), every], load_sem.at[0])
    own_copy.start()
    small_copies = [
        pltpu.make_async_copy(source, target, load_sem.at[3 + groups + i])
        for i, (source, target) in enumerate((
            (scales_hbm, scales_ref), (counts_hbm, counts_ref),
            (gate_scales_hbm, gate_scales_ref), (up_scales_hbm, up_scales_ref),
        ))
    ]
    for copy in small_copies:
        copy.start()
    gate_copy = pltpu.make_async_copy(gate_hbm, weights.at[pl.ds(0, units)], load_sem.at[1])
    gate_copy.start()
    up_copy = pltpu.make_async_copy(up_hbm, weights.at[pl.ds(units, units)], load_sem.at[2])
    up_copy.start()
    small_copies[0].wait()
    small_copies[1].wait()
    kept = equal_ids(SLOTS, SLOTS) & (lax.broadcasted_iota(jnp.int32, (SLOTS, SLOTS), 0) < counts_ref[0])
    spread = jnp.where(kept, scales_ref[...].astype(jnp.float32), 0.0)
    scale_col = jnp.sum(spread, axis=1, keepdims=True)
    rows_buf[rows_of(me), pl.ds(width, EXTRA)] = jnp.broadcast_to(scale_col, (SLOTS, EXTRA)).astype(jnp.bfloat16)
    own_peaks[...] = jnp.zeros_like(own_peaks)
    all_peaks[...] = jnp.zeros_like(all_peaks)
    own_copy.wait()
    pl.semaphore_wait(barrier, 3)

    def remote(span, columns, send, recv, device):
        part = rows_buf.at[span, columns]
        return pltpu.make_async_remote_copy(
            src_ref=part, dst_ref=part, send_sem=send, recv_sem=recv,
            device_id={"tp": device}, device_id_type=MESH,
        )

    def ring(hop, s):
        return remote(block(hop - 1), piece(s, core), send_sem.at[hop, s], recv_sem.at[hop, s], ahead)

    def own(way, s):
        server = core if way == 0 else 1 - core
        device = ahead if way == 0 else across
        return remote(rows_of(me), piece(s, server), send_sem.at[way, s], recv_sem.at[way, s], device)

    def share(hop, s):
        columns = pl.ds(0, full) if hop < far else piece(s, core)
        return remote(block(hop), columns, sib_send.at[hop, s], sib_recv.at[hop, s], sibling)

    def shares_at(hop):
        return 1 if hop < far else PIECES // 2

    own_share = remote(rows_of(me), pl.ds(0, full), sib_send.at[0, 0], sib_recv.at[0, 0], sibling)

    def pieces_at(hop):
        return PIECES if hop < far else PIECES // 2

    def wait_shared(hop):
        if hop == 0:
            own_share.wait_recv()
        else:
            for s in range(shares_at(hop)):
                share(hop, s).wait_recv()

    first = chip // group_chips
    nearer = 2 * (lax.rem(chip, group_chips) // (group_chips // 2)) - 1
    ranked = [lax.rem(first + groups + step, groups) for step in (0, nearer, -nearer, 2)]

    low = lax.rem(first + 1 + (nearer + 1) // 2, groups)
    late_pair, early_pair = pl.ds(low, 2), pl.ds(low + 2, 2)

    def spans_of(picked):
        return [pl.ds(pl.multiple_of(ranked[i] * LANES, LANES), LANES) for i in picked]

    def out_copy(i):
        span = spans_of((i,))[0]
        return pltpu.make_async_copy(hidden_buf.at[:, span], hidden_hbm.at[:, span], load_sem.at[3 + i])

    def multiply(picked, part, depth):
        x = jnp.concatenate([rows_buf[span, depth] for span in spans_of(picked)], axis=0)
        return lax.dot_general(
            weights[pl.ds(part * units, units), depth], x, (((1,), (1,)), ((), ())),
            preferred_element_type=jnp.float32,
        )

    def finish(picked, gates, ups):
        for i, span in enumerate(spans_of(picked)):
            spread = jnp.where(equal_ids(LANES, LANES), rows_buf[span, pl.ds(width, LANES)].astype(jnp.float32), 0.0)
            scale = jnp.sum(spread, axis=0, keepdims=True)
            lanes = slice(i * LANES, (i + 1) * LANES)
            gate = gates[:, lanes] * scale * channel_scales[:, 0:1]
            up = ups[:, lanes] * scale * channel_scales[:, 1:2]
            hidden = (gate / (1.0 + jnp.exp(-gate)) * up).astype(jnp.bfloat16)
            hidden_buf[:, span] = hidden
            out_copy(picked[i]).start()
            peak = jnp.max(jnp.abs(hidden.astype(jnp.float32)), axis=0, keepdims=True)
            own_peaks[low + lax.rem(ranked[picked[i]] - low + groups, groups), :, :] = peak

    swap = pltpu.make_async_remote_copy(
        src_ref=own_peaks.at[early_pair], dst_ref=sibling_peaks, send_sem=early_send.at[0], recv_sem=early_recv.at[0],
        device_id={"tp": sibling}, device_id_type=MESH,
    )

    for s in range(PIECES):
        own(0, s).start()
        own(1, s).start()
    own_share.start()
    for hop in range(1, far + 1):
        for s in range(pieces_at(hop)):
            if hop == 1:
                own(0, s).wait_recv()
                own(1, s).wait_recv()
            else:
                ring(hop, s).wait_recv()
            if hop < far and s < pieces_at(hop + 1):
                ring(hop + 1, s).start()
            if hop == far or s == PIECES - 1:
                share(hop, 0 if hop < far else s).start()
        if hop == 1:
            small_copies[2].wait()
            small_copies[3].wait()
            for k, ref in enumerate((gate_scales_ref, up_scales_ref)):
                spread = jnp.where(equal_ids(units, units), ref[...].reshape(1, units), 0.0)
                channel_scales[:, k:k + 1] = jnp.sum(spread, axis=1, keepdims=True)
        elif hop == 6:
            gate_copy.wait()
            up_copy.wait()
            for earlier in range(6):
                wait_shared(earlier)
            early_gates[...] = multiply((0, 1), 0, every)
        elif hop == 7:
            finish((0, 1), early_gates[...], multiply((0, 1), 1, every))
            swap.start()

    def peak_copy(step, pair, send, recv):
        return pltpu.make_async_remote_copy(
            src_ref=own_peaks.at[pair],
            dst_ref=all_peaks.at[step - 1, pair],
            send_sem=send.at[step - 1],
            recv_sem=recv.at[step - 1],
            device_id={"tp": lax.rem(me + step, tp)},
            device_id_type=MESH,
        )

    def early(step):
        return peak_copy(step, early_pair, early_send, early_recv)

    def late(step):
        return peak_copy(step, late_pair, peak_send, peak_recv)

    order = sorted(range(1, tp), key=lambda step: -min(step, tp - step))
    wait_shared(6)
    wait_shared(7)
    swap.wait()
    own_peaks[early_pair, :, :] = jnp.maximum(own_peaks[early_pair, :, :], sibling_peaks[...])
    for step in order:
        if step % 2 == 0:
            early(step).start()
    wait_shared(8)
    finish((2, 3), multiply((2, 3), 0, every), multiply((2, 3), 1, every))
    for step in order:
        late(step).start()
    own_share.wait_send()
    for hop in range(1, far + 1):
        for s in range(pieces_at(hop)):
            if hop == 1:
                own(0, s).wait_send()
                own(1, s).wait_send()
            else:
                ring(hop, s).wait_send()
        for s in range(shares_at(hop)):
            share(hop, s).wait_send()
    for i in range(groups):
        out_copy(i).wait()
    for step in reversed(order):
        if step % 2 == 0:
            early(step).wait()
        late(step).wait()
    peaks = jnp.maximum(jnp.max(all_peaks[...], axis=0), own_peaks[...])
    for g in range(groups):
        peaks_ref[g:g + 1, :] = jnp.maximum(jnp.maximum(peaks[g], peaks[g + groups]), 1e-5)


def normalise(hidden_ref, peaks_ref, down_ref, row_peak_ref):
    for g in range(peaks_ref.shape[0]):
        span = slice(g * LANES, (g + 1) * LANES)
        peak = peaks_ref[g:g + 1, :]
        down_ref[:, span] = (hidden_ref[:, span].astype(jnp.float32) / peak).astype(jnp.bfloat16)
        row_peak_ref[span] = peak.reshape(LANES)


def shards(token_codes, token_scales, live_counts, gate_codes, up_codes, gate_scales, up_scales):
    tp = lax.axis_size("tp")
    width = token_codes.shape[1]
    units = gate_codes.shape[1]
    row_count = tp * SLOTS
    groups = row_count // LANES
    whole = pl.BlockSpec(memory_space=pltpu.VMEM)
    hbm = pl.BlockSpec(memory_space=pltpu.HBM)
    far = tp // 4
    dma = pltpu.SemaphoreType.DMA
    hidden, peaks = pl.pallas_call(
        functools.partial(kernel, tp, width, units),
        out_shape=(
            jax.ShapeDtypeStruct((units, row_count), jnp.bfloat16),
            jax.ShapeDtypeStruct((groups, LANES), jnp.float32),
        ),
        in_specs=[hbm] * 7,
        out_specs=(hbm, whole),
        scratch_shapes=[
            pltpu.VMEM((units, row_count), jnp.bfloat16),
            pltpu.VMEM((row_count, width + EXTRA), jnp.bfloat16),
            pltpu.VMEM((2 * units, width), jnp.bfloat16),
            pltpu.VMEM((units, 2 * LANES), jnp.float32),
            pltpu.VMEM((units, LANES), jnp.float32),
            pltpu.VMEM((2 * groups, 1, LANES), jnp.float32),
            pltpu.VMEM((tp - 1, 2 * groups, 1, LANES), jnp.float32),
            pltpu.VMEM((2, 1, LANES), jnp.float32),
            pltpu.VMEM((1, SLOTS), jnp.bfloat16),
            pltpu.SMEM((1,), jnp.int32),
            pltpu.VMEM((units,), jnp.float32),
            pltpu.VMEM((units,), jnp.float32),
            dma((far + 1, PIECES)),
            dma((far + 1, PIECES)),
            dma((far + 1, PIECES)),
            dma((far + 1, PIECES)),
            dma((tp - 1,)),
            dma((tp - 1,)),
            dma((tp - 1,)),
            dma((tp - 1,)),
            dma((7 + groups,)),
        ],
        compiler_params=pltpu.CompilerParams(
            collective_id=0, has_side_effects=True, vmem_limit_bytes=60 << 20
        ),
    )(
        token_codes, token_scales[None, :], live_counts, gate_codes.T, up_codes.T,
        gate_scales, up_scales,
    )
    down_input, row_peak = pl.pallas_call(
        normalise,
        out_shape=(
            jax.ShapeDtypeStruct((units, row_count), jnp.bfloat16),
            jax.ShapeDtypeStruct((row_count,), jnp.float32),
        ),
        in_specs=[whole, whole],
        out_specs=(whole, whole),
    )(hidden, peaks)
    return (down_input.T, row_peak)


def solution(mesh):
    in_specs = (
        P(("dp", "tp"), None),
        P(("dp", "tp")),
        P(("dp", "tp")),
        P(None, "tp"),
        P(None, "tp"),
        P("tp"),
        P("tp"),
    )
    out_specs = (P("dp", "tp"), P("dp"))
    return jax.shard_map(shards, mesh=mesh, in_specs=in_specs, out_specs=out_specs, check_vma=False)
```

```python
import functools

import jax
import jax.numpy as jnp
from jax import lax
from jax.experimental import pallas as pl
from jax.experimental.pallas import tpu as pltpu
from jax.sharding import PartitionSpec as P

MESH = pl.DeviceIdType.MESH
SLOTS = 16
PIECES = 6
LANES = 128
EXTRA = 2 * LANES


def equal_ids(rows, columns):
    shape = (rows, columns)
    return lax.broadcasted_iota(jnp.int32, shape, 0) == lax.broadcasted_iota(jnp.int32, shape, 1)


def kernel(
    tp, width, units,
    codes_hbm, scales_hbm, counts_hbm, gate_hbm, up_hbm, gate_scales_hbm, up_scales_hbm,
    hidden_hbm, peaks_ref,
    hidden_buf, rows_buf, weights, early_gates, channel_scales, own_peaks, all_peaks, sibling_peaks,
    scales_ref, counts_ref, gate_scales_ref, up_scales_ref,
    send_sem, recv_sem, sib_send, sib_recv, peak_send, peak_recv, early_send, early_recv, load_sem,
):
    me = lax.axis_index("tp")
    chips = tp // 2
    far = chips // 2
    core = lax.rem(me, 2)
    sibling = me + 1 - 2 * core
    chip = me // 2
    groups = tp * SLOTS // LANES
    group_chips = chips // groups
    full = width + EXTRA
    every = pl.ds(0, width)

    toward = 1 - 2 * core
    ahead = lax.rem(me + 2 * toward + tp, tp)
    behind = lax.rem(me - 2 * toward + tp, tp)
    across = lax.rem(sibling - 2 * toward + tp, tp)

    def rows_of(device):
        return pl.ds(pl.multiple_of(device * SLOTS, SLOTS), SLOTS)

    def block(hop):
        start = lax.rem(chip - toward * hop + chips, chips) * (2 * SLOTS)
        return pl.ds(pl.multiple_of(start, 2 * SLOTS), 2 * SLOTS)

    def piece(s, server):
        index = lax.rem(s + server * (PIECES // 2), PIECES)
        return pl.ds(pl.multiple_of(index * (full // PIECES), LANES), full // PIECES)

    barrier = pltpu.get_barrier_semaphore()
    for device in (behind, across, sibling):
        pl.semaphore_signal(barrier, inc=1, device_id={"tp": device}, device_id_type=MESH)
    own_copy = pltpu.make_async_copy(codes_hbm, rows_buf.at[rows_of(me), every], load_sem.at[0])
    own_copy.start()
    small_copies = [
        pltpu.make_async_copy(source, target, load_sem.at[3 + groups + i])
        for i, (source, target) in enumerate((
            (scales_hbm, scales_ref), (counts_hbm, counts_ref),
            (gate_scales_hbm, gate_scales_ref), (up_scales_hbm, up_scales_ref),
        ))
    ]
    for copy in small_copies:
        copy.start()
    gate_copy = pltpu.make_async_copy(gate_hbm, weights.at[pl.ds(0, units)], load_sem.at[1])
    gate_copy.start()
    up_copy = pltpu.make_async_copy(up_hbm, weights.at[pl.ds(units, units)], load_sem.at[2])
    up_copy.start()
    small_copies[0].wait()
    small_copies[1].wait()
    kept = equal_ids(SLOTS, SLOTS) & (lax.broadcasted_iota(jnp.int32, (SLOTS, SLOTS), 0) < counts_ref[0])
    spread = jnp.where(kept, scales_ref[...].astype(jnp.float32), 0.0)
    scale_col = jnp.sum(spread, axis=1, keepdims=True)
    rows_buf[rows_of(me), pl.ds(width, EXTRA)] = jnp.broadcast_to(scale_col, (SLOTS, EXTRA)).astype(jnp.bfloat16)
    own_peaks[...] = jnp.zeros_like(own_peaks)
    all_peaks[...] = jnp.zeros_like(all_peaks)
    own_copy.wait()
    pl.semaphore_wait(barrier, 3)

    def remote(span, columns, send, recv, device):
        part = rows_buf.at[span, columns]
        return pltpu.make_async_remote_copy(
            src_ref=part, dst_ref=part, send_sem=send, recv_sem=recv,
            device_id={"tp": device}, device_id_type=MESH,
        )

    def ring(hop, s):
        return remote(block(hop - 1), piece(s, core), send_sem.at[hop, s], recv_sem.at[hop, s], ahead)

    def own(way, s):
        server = core if way == 0 else 1 - core
        device = ahead if way == 0 else across
        return remote(rows_of(me), piece(s, server), send_sem.at[way, s], recv_sem.at[way, s], device)

    def share(hop, s):
        columns = pl.ds(0, full) if hop < far else piece(s, core)
        return remote(block(hop), columns, sib_send.at[hop, s], sib_recv.at[hop, s], sibling)

    def shares_at(hop):
        return 1 if hop < far else PIECES // 2

    own_share = remote(rows_of(me), pl.ds(0, full), sib_send.at[0, 0], sib_recv.at[0, 0], sibling)

    def pieces_at(hop):
        return PIECES if hop < far else PIECES // 2

    def wait_shared(hop):
        if hop == 0:
            own_share.wait_recv()
        else:
            for s in range(shares_at(hop)):
                share(hop, s).wait_recv()

    first = chip // group_chips
    nearer = 2 * (lax.rem(chip, group_chips) // (group_chips // 2)) - 1
    ranked = [lax.rem(first + groups + step, groups) for step in (0, nearer, -nearer, 2)]

    low = lax.rem(first + 1 + (nearer + 1) // 2, groups)
    late_pair, early_pair = pl.ds(low, 2), pl.ds(low + 2, 2)

    def spans_of(picked):
        return [pl.ds(pl.multiple_of(ranked[i] * LANES, LANES), LANES) for i in picked]

    def out_copy(i):
        span = spans_of((i,))[0]
        return pltpu.make_async_copy(hidden_buf.at[:, span], hidden_hbm.at[:, span], load_sem.at[3 + i])

    def multiply(picked, part, depth):
        x = jnp.concatenate([rows_buf[span, depth] for span in spans_of(picked)], axis=0)
        return lax.dot_general(
            weights[pl.ds(part * units, units), depth], x, (((1,), (1,)), ((), ())),
            preferred_element_type=jnp.float32,
        )

    def finish(picked, gates, ups):
        for i, span in enumerate(spans_of(picked)):
            spread = jnp.where(equal_ids(LANES, LANES), rows_buf[span, pl.ds(width, LANES)].astype(jnp.float32), 0.0)
            scale = jnp.sum(spread, axis=0, keepdims=True)
            lanes = slice(i * LANES, (i + 1) * LANES)
            gate = gates[:, lanes] * scale * channel_scales[:, 0:1]
            up = ups[:, lanes] * scale * channel_scales[:, 1:2]
            hidden = (gate / (1.0 + jnp.exp(-gate)) * up).astype(jnp.bfloat16)
            hidden_buf[:, span] = hidden
            out_copy(picked[i]).start()
            peak = jnp.max(jnp.abs(hidden.astype(jnp.float32)), axis=0, keepdims=True)
            own_peaks[low + lax.rem(ranked[picked[i]] - low + groups, groups), :, :] = peak

    swap = pltpu.make_async_remote_copy(
        src_ref=own_peaks.at[early_pair], dst_ref=sibling_peaks, send_sem=early_send.at[0], recv_sem=early_recv.at[0],
        device_id={"tp": sibling}, device_id_type=MESH,
    )

    def peak_copy(step, pair, send, recv):
        return pltpu.make_async_remote_copy(
            src_ref=own_peaks.at[pair],
            dst_ref=all_peaks.at[step - 1, pair],
            send_sem=send.at[step - 1],
            recv_sem=recv.at[step - 1],
            device_id={"tp": lax.rem(me + step, tp)},
            device_id_type=MESH,
        )

    def early(step):
        return peak_copy(step, early_pair, early_send, early_recv)

    def late(step):
        return peak_copy(step, late_pair, peak_send, peak_recv)

    order = sorted(range(1, tp), key=lambda step: -min(step, tp - step))
    for s in range(PIECES):
        own(0, s).start()
        own(1, s).start()
    own_share.start()
    for hop in range(1, far + 1):
        for s in range(pieces_at(hop)):
            if hop == 1:
                own(0, s).wait_recv()
                own(1, s).wait_recv()
            else:
                ring(hop, s).wait_recv()
            if hop < far and s < pieces_at(hop + 1):
                ring(hop + 1, s).start()
            if hop == far or s == PIECES - 1:
                share(hop, 0 if hop < far else s).start()
        if hop == 1:
            small_copies[2].wait()
            small_copies[3].wait()
            for k, ref in enumerate((gate_scales_ref, up_scales_ref)):
                spread = jnp.where(equal_ids(units, units), ref[...].reshape(1, units), 0.0)
                channel_scales[:, k:k + 1] = jnp.sum(spread, axis=1, keepdims=True)
        elif hop == 6:
            gate_copy.wait()
            up_copy.wait()
            for earlier in range(6):
                wait_shared(earlier)
            finish((0, 1), multiply((0, 1), 0, every), multiply((0, 1), 1, every))
            swap.start()
        elif hop == 7:
            swap.wait()
            own_peaks[early_pair, :, :] = jnp.maximum(own_peaks[early_pair, :, :], sibling_peaks[...])
            wait_shared(6)
            for step in order:
                if step % 2 == 0 and min(step, tp - step) // 2 <= 6:
                    early(step).start()

    wait_shared(7)
    for step in order:
        if step % 2 == 0 and min(step, tp - step) // 2 > 6:
            early(step).start()
    wait_shared(8)
    finish((2, 3), multiply((2, 3), 0, every), multiply((2, 3), 1, every))
    for step in order:
        late(step).start()
    own_share.wait_send()
    for hop in range(1, far + 1):
        for s in range(pieces_at(hop)):
            if hop == 1:
                own(0, s).wait_send()
                own(1, s).wait_send()
            else:
                ring(hop, s).wait_send()
        for s in range(shares_at(hop)):
            share(hop, s).wait_send()
    for i in range(groups):
        out_copy(i).wait()
    for step in reversed(order):
        if step % 2 == 0:
            early(step).wait()
        late(step).wait()
    peaks = jnp.maximum(jnp.max(all_peaks[...], axis=0), own_peaks[...])
    for g in range(groups):
        peaks_ref[g:g + 1, :] = jnp.maximum(jnp.maximum(peaks[g], peaks[g + groups]), 1e-5)


def normalise(hidden_ref, peaks_ref, down_ref, row_peak_ref):
    for g in range(peaks_ref.shape[0]):
        span = slice(g * LANES, (g + 1) * LANES)
        peak = peaks_ref[g:g + 1, :]
        down_ref[:, span] = (hidden_ref[:, span].astype(jnp.float32) / peak).astype(jnp.bfloat16)
        row_peak_ref[span] = peak.reshape(LANES)


def shards(token_codes, token_scales, live_counts, gate_codes, up_codes, gate_scales, up_scales):
    tp = lax.axis_size("tp")
    width = token_codes.shape[1]
    units = gate_codes.shape[1]
    row_count = tp * SLOTS
    groups = row_count // LANES
    whole = pl.BlockSpec(memory_space=pltpu.VMEM)
    hbm = pl.BlockSpec(memory_space=pltpu.HBM)
    far = tp // 4
    dma = pltpu.SemaphoreType.DMA
    hidden, peaks = pl.pallas_call(
        functools.partial(kernel, tp, width, units),
        out_shape=(
            jax.ShapeDtypeStruct((units, row_count), jnp.bfloat16),
            jax.ShapeDtypeStruct((groups, LANES), jnp.float32),
        ),
        in_specs=[hbm] * 7,
        out_specs=(hbm, whole),
        scratch_shapes=[
            pltpu.VMEM((units, row_count), jnp.bfloat16),
            pltpu.VMEM((row_count, width + EXTRA), jnp.bfloat16),
            pltpu.VMEM((2 * units, width), jnp.bfloat16),
            pltpu.VMEM((units, 2 * LANES), jnp.float32),
            pltpu.VMEM((units, LANES), jnp.float32),
            pltpu.VMEM((2 * groups, 1, LANES), jnp.float32),
            pltpu.VMEM((tp - 1, 2 * groups, 1, LANES), jnp.float32),
            pltpu.VMEM((2, 1, LANES), jnp.float32),
            pltpu.VMEM((1, SLOTS), jnp.bfloat16),
            pltpu.SMEM((1,), jnp.int32),
            pltpu.VMEM((units,), jnp.float32),
            pltpu.VMEM((units,), jnp.float32),
            dma((far + 1, PIECES)),
            dma((far + 1, PIECES)),
            dma((far + 1, PIECES)),
            dma((far + 1, PIECES)),
            dma((tp - 1,)),
            dma((tp - 1,)),
            dma((tp - 1,)),
            dma((tp - 1,)),
            dma((7 + groups,)),
        ],
        compiler_params=pltpu.CompilerParams(
            collective_id=0, has_side_effects=True, vmem_limit_bytes=60 << 20
        ),
    )(
        token_codes, token_scales[None, :], live_counts, gate_codes.T, up_codes.T,
        gate_scales, up_scales,
    )
    down_input, row_peak = pl.pallas_call(
        normalise,
        out_shape=(
            jax.ShapeDtypeStruct((units, row_count), jnp.bfloat16),
            jax.ShapeDtypeStruct((row_count,), jnp.float32),
        ),
        in_specs=[whole, whole],
        out_specs=(whole, whole),
    )(hidden, peaks)
    return (down_input.T, row_peak)


def solution(mesh):
    in_specs = (
        P(("dp", "tp"), None),
        P(("dp", "tp")),
        P(("dp", "tp")),
        P(None, "tp"),
        P(None, "tp"),
        P("tp"),
        P("tp"),
    )
    out_specs = (P("dp", "tp"), P("dp"))
    return jax.shard_map(shards, mesh=mesh, in_specs=in_specs, out_specs=out_specs, check_vma=False)
```

```python
import functools

import jax
import jax.numpy as jnp
from jax import lax
from jax.experimental import pallas as pl
from jax.experimental.pallas import tpu as pltpu
from jax.sharding import PartitionSpec as P

MESH = pl.DeviceIdType.MESH
SLOTS = 16
PIECES = 6
LANES = 128
EXTRA = 2 * LANES


def equal_ids(rows, columns):
    shape = (rows, columns)
    return lax.broadcasted_iota(jnp.int32, shape, 0) == lax.broadcasted_iota(jnp.int32, shape, 1)


def kernel(
    tp, width, units,
    codes_hbm, scales_hbm, counts_hbm, gate_hbm, up_hbm, gate_scales_hbm, up_scales_hbm,
    hidden_hbm, peaks_ref,
    hidden_buf, rows_buf, weights, channel_scales, own_peaks, all_peaks, sibling_peaks,
    scales_ref, counts_ref, gate_scales_ref, up_scales_ref,
    send_sem, recv_sem, sib_send, sib_recv, peak_send, peak_recv, early_send, early_recv, load_sem,
):
    me = lax.axis_index("tp")
    chips = tp // 2
    far = chips // 2
    core = lax.rem(me, 2)
    sibling = me + 1 - 2 * core
    chip = me // 2
    groups = tp * SLOTS // LANES
    group_chips = chips // groups
    full = width + EXTRA
    every = pl.ds(0, width)

    toward = 1 - 2 * core
    ahead = lax.rem(me + 2 * toward + tp, tp)
    behind = lax.rem(me - 2 * toward + tp, tp)
    across = lax.rem(sibling - 2 * toward + tp, tp)

    def rows_of(device):
        return pl.ds(pl.multiple_of(device * SLOTS, SLOTS), SLOTS)

    def block(hop):
        start = lax.rem(chip - toward * hop + chips, chips) * (2 * SLOTS)
        return pl.ds(pl.multiple_of(start, 2 * SLOTS), 2 * SLOTS)

    def piece(s, server):
        index = lax.rem(s + server * (PIECES // 2), PIECES)
        return pl.ds(pl.multiple_of(index * (full // PIECES), LANES), full // PIECES)

    barrier = pltpu.get_barrier_semaphore()
    for device in (behind, across, sibling):
        pl.semaphore_signal(barrier, inc=1, device_id={"tp": device}, device_id_type=MESH)
    own_copy = pltpu.make_async_copy(codes_hbm, rows_buf.at[rows_of(me), every], load_sem.at[0])
    own_copy.start()
    small_copies = [
        pltpu.make_async_copy(source, target, load_sem.at[3 + groups + i])
        for i, (source, target) in enumerate((
            (scales_hbm, scales_ref), (counts_hbm, counts_ref),
            (gate_scales_hbm, gate_scales_ref), (up_scales_hbm, up_scales_ref),
        ))
    ]
    for copy in small_copies:
        copy.start()
    gate_copy = pltpu.make_async_copy(gate_hbm, weights.at[pl.ds(0, units)], load_sem.at[1])
    gate_copy.start()
    up_copy = pltpu.make_async_copy(up_hbm, weights.at[pl.ds(units, units)], load_sem.at[2])
    up_copy.start()
    small_copies[0].wait()
    small_copies[1].wait()
    kept = equal_ids(SLOTS, SLOTS) & (lax.broadcasted_iota(jnp.int32, (SLOTS, SLOTS), 0) < counts_ref[0])
    spread = jnp.where(kept, scales_ref[...].astype(jnp.float32), 0.0)
    scale_col = jnp.sum(spread, axis=1, keepdims=True)
    rows_buf[rows_of(me), pl.ds(width, EXTRA)] = jnp.broadcast_to(scale_col, (SLOTS, EXTRA)).astype(jnp.bfloat16)
    own_peaks[...] = jnp.zeros_like(own_peaks)
    all_peaks[...] = jnp.zeros_like(all_peaks)
    own_copy.wait()
    pl.semaphore_wait(barrier, 3)

    def remote(span, columns, send, recv, device):
        part = rows_buf.at[span, columns]
        return pltpu.make_async_remote_copy(
            src_ref=part, dst_ref=part, send_sem=send, recv_sem=recv,
            device_id={"tp": device}, device_id_type=MESH,
        )

    def ring(hop, s):
        return remote(block(hop - 1), piece(s, core), send_sem.at[hop, s], recv_sem.at[hop, s], ahead)

    def own(way, s):
        server = core if way == 0 else 1 - core
        device = ahead if way == 0 else across
        return remote(rows_of(me), piece(s, server), send_sem.at[way, s], recv_sem.at[way, s], device)

    def share(hop, s):
        columns = pl.ds(0, full) if hop < far else piece(s, core)
        return remote(block(hop), columns, sib_send.at[hop, s], sib_recv.at[hop, s], sibling)

    def shares_at(hop):
        return 1 if hop < far else PIECES // 2

    own_share = remote(rows_of(me), pl.ds(0, full), sib_send.at[0, 0], sib_recv.at[0, 0], sibling)

    def pieces_at(hop):
        return PIECES if hop < far else PIECES // 2

    def wait_shared(hop):
        if hop == 0:
            own_share.wait_recv()
        else:
            for s in range(shares_at(hop)):
                share(hop, s).wait_recv()

    first = chip // group_chips
    nearer = 2 * (lax.rem(chip, group_chips) // (group_chips // 2)) - 1
    ranked = [lax.rem(first + groups + step, groups) for step in (0, nearer, -nearer, 2)]

    low = lax.rem(first + 1 + (nearer + 1) // 2, groups)
    late_pair, early_pair = pl.ds(low, 2), pl.ds(low + 2, 2)

    def spans_of(picked):
        return [pl.ds(pl.multiple_of(ranked[i] * LANES, LANES), LANES) for i in picked]

    def out_copy(i):
        span = spans_of((i,))[0]
        return pltpu.make_async_copy(hidden_buf.at[:, span], hidden_hbm.at[:, span], load_sem.at[3 + i])

    def multiply(picked, part, depth):
        x = jnp.concatenate([rows_buf[span, depth] for span in spans_of(picked)], axis=0)
        return lax.dot_general(
            weights[pl.ds(part * units, units), depth], x, (((1,), (1,)), ((), ())),
            preferred_element_type=jnp.float32,
        )

    def finish(picked, gates, ups):
        for i, span in enumerate(spans_of(picked)):
            spread = jnp.where(equal_ids(LANES, LANES), rows_buf[span, pl.ds(width, LANES)].astype(jnp.float32), 0.0)
            scale = jnp.sum(spread, axis=0, keepdims=True)
            lanes = slice(i * LANES, (i + 1) * LANES)
            gate = gates[:, lanes] * scale * channel_scales[:, 0:1]
            up = ups[:, lanes] * scale * channel_scales[:, 1:2]
            hidden = (gate / (1.0 + jnp.exp(-gate)) * up).astype(jnp.bfloat16)
            hidden_buf[:, span] = hidden
            out_copy(picked[i]).start()
            peak = jnp.max(jnp.abs(hidden.astype(jnp.float32)), axis=0, keepdims=True)
            own_peaks[low + lax.rem(ranked[picked[i]] - low + groups, groups), :, :] = peak

    swap = pltpu.make_async_remote_copy(
        src_ref=own_peaks.at[early_pair], dst_ref=sibling_peaks, send_sem=early_send.at[0], recv_sem=early_recv.at[0],
        device_id={"tp": sibling}, device_id_type=MESH,
    )

    for s in range(PIECES):
        own(0, s).start()
        own(1, s).start()
    own_share.start()
    for hop in range(1, far + 1):
        for s in range(pieces_at(hop)):
            if hop == 1:
                own(0, s).wait_recv()
                own(1, s).wait_recv()
            else:
                ring(hop, s).wait_recv()
            if hop < far and s < pieces_at(hop + 1):
                ring(hop + 1, s).start()
            if hop == far or s == PIECES - 1:
                share(hop, 0 if hop < far else s).start()
        if hop == 1:
            small_copies[2].wait()
            small_copies[3].wait()
            for k, ref in enumerate((gate_scales_ref, up_scales_ref)):
                spread = jnp.where(equal_ids(units, units), ref[...].reshape(1, units), 0.0)
                channel_scales[:, k:k + 1] = jnp.sum(spread, axis=1, keepdims=True)
        elif hop == 7:
            gate_copy.wait()
            up_copy.wait()
            for earlier in range(6):
                wait_shared(earlier)
            finish((0, 1), multiply((0, 1), 0, every), multiply((0, 1), 1, every))
            swap.start()

    def peak_copy(step, pair, send, recv):
        return pltpu.make_async_remote_copy(
            src_ref=own_peaks.at[pair],
            dst_ref=all_peaks.at[step - 1, pair],
            send_sem=send.at[step - 1],
            recv_sem=recv.at[step - 1],
            device_id={"tp": lax.rem(me + step, tp)},
            device_id_type=MESH,
        )

    def early(step):
        return peak_copy(step, early_pair, early_send, early_recv)

    def late(step):
        return peak_copy(step, late_pair, peak_send, peak_recv)

    order = sorted(range(1, tp), key=lambda step: -min(step, tp - step))
    wait_shared(6)
    wait_shared(7)
    swap.wait()
    own_peaks[early_pair, :, :] = jnp.maximum(own_peaks[early_pair, :, :], sibling_peaks[...])
    for step in order:
        if step % 2 == 0:
            early(step).start()
    wait_shared(8)
    finish((2, 3), multiply((2, 3), 0, every), multiply((2, 3), 1, every))
    for step in order:
        late(step).start()
    own_share.wait_send()
    for hop in range(1, far + 1):
        for s in range(pieces_at(hop)):
            if hop == 1:
                own(0, s).wait_send()
                own(1, s).wait_send()
            else:
                ring(hop, s).wait_send()
        for s in range(shares_at(hop)):
            share(hop, s).wait_send()
    for i in range(groups):
        out_copy(i).wait()
    for step in reversed(order):
        if step % 2 == 0:
            early(step).wait()
        late(step).wait()
    peaks = jnp.maximum(jnp.max(all_peaks[...], axis=0), own_peaks[...])
    for g in range(groups):
        peaks_ref[g:g + 1, :] = jnp.maximum(jnp.maximum(peaks[g], peaks[g + groups]), 1e-5)


def normalise(hidden_ref, peaks_ref, down_ref, row_peak_ref):
    for g in range(peaks_ref.shape[0]):
        span = slice(g * LANES, (g + 1) * LANES)
        peak = peaks_ref[g:g + 1, :]
        down_ref[:, span] = (hidden_ref[:, span].astype(jnp.float32) / peak).astype(jnp.bfloat16)
        row_peak_ref[span] = peak.reshape(LANES)


def shards(token_codes, token_scales, live_counts, gate_codes, up_codes, gate_scales, up_scales):
    tp = lax.axis_size("tp")
    width = token_codes.shape[1]
    units = gate_codes.shape[1]
    row_count = tp * SLOTS
    groups = row_count // LANES
    whole = pl.BlockSpec(memory_space=pltpu.VMEM)
    hbm = pl.BlockSpec(memory_space=pltpu.HBM)
    far = tp // 4
    dma = pltpu.SemaphoreType.DMA
    hidden, peaks = pl.pallas_call(
        functools.partial(kernel, tp, width, units),
        out_shape=(
            jax.ShapeDtypeStruct((units, row_count), jnp.bfloat16),
            jax.ShapeDtypeStruct((groups, LANES), jnp.float32),
        ),
        in_specs=[hbm] * 7,
        out_specs=(hbm, whole),
        scratch_shapes=[
            pltpu.VMEM((units, row_count), jnp.bfloat16),
            pltpu.VMEM((row_count, width + EXTRA), jnp.bfloat16),
            pltpu.VMEM((2 * units, width), jnp.bfloat16),
            pltpu.VMEM((units, LANES), jnp.float32),
            pltpu.VMEM((2 * groups, 1, LANES), jnp.float32),
            pltpu.VMEM((tp - 1, 2 * groups, 1, LANES), jnp.float32),
            pltpu.VMEM((2, 1, LANES), jnp.float32),
            pltpu.VMEM((1, SLOTS), jnp.bfloat16),
            pltpu.SMEM((1,), jnp.int32),
            pltpu.VMEM((units,), jnp.float32),
            pltpu.VMEM((units,), jnp.float32),
            dma((far + 1, PIECES)),
            dma((far + 1, PIECES)),
            dma((far + 1, PIECES)),
            dma((far + 1, PIECES)),
            dma((tp - 1,)),
            dma((tp - 1,)),
            dma((tp - 1,)),
            dma((tp - 1,)),
            dma((7 + groups,)),
        ],
        compiler_params=pltpu.CompilerParams(
            collective_id=0, has_side_effects=True, vmem_limit_bytes=60 << 20
        ),
    )(
        token_codes, token_scales[None, :], live_counts, gate_codes.T, up_codes.T,
        gate_scales, up_scales,
    )
    down_input, row_peak = pl.pallas_call(
        normalise,
        out_shape=(
            jax.ShapeDtypeStruct((units, row_count), jnp.bfloat16),
            jax.ShapeDtypeStruct((row_count,), jnp.float32),
        ),
        in_specs=[whole, whole],
        out_specs=(whole, whole),
    )(hidden, peaks)
    return (down_input.T, row_peak)


def solution(mesh):
    in_specs = (
        P(("dp", "tp"), None),
        P(("dp", "tp")),
        P(("dp", "tp")),
        P(None, "tp"),
        P(None, "tp"),
        P("tp"),
        P("tp"),
    )
    out_specs = (P("dp", "tp"), P("dp"))
    return jax.shard_map(shards, mesh=mesh, in_specs=in_specs, out_specs=out_specs, check_vma=False)
```
